32 devices in a mesh: section: 4 (over z), tensor: 8 (over y, x, core).
Axes of the slice: x: 2, y: 2, z: 4, core: 2. Of those that a mesh axis runs over, the one named last changes fastest.
Arguments:
- dy_top: bfloat16 [2, 64, 8192], replicated, may hold values from -6 to 6
- loss_mask: int32 [2, 64], replicated, may hold values 0 or 1
- counts: int32 [2], replicated, may hold values from 8 to 64, as said below
- layer_in: bfloat16 [4, 2, 64, 8192], P('section'), may hold values from -60 to 60
- conv_in: bfloat16 [4, 2, 64, 10240], P('section', None, None, 'tensor'), may hold values from -6 to 6
- norm_gain: float32 [4, 8192], P('section'), may hold values from 0.3 to 3
- conv_weight: float32 [4, 4, 10240], P('section', None, 'tensor'), may hold values from -2.5 to 2.5
- in_proj: bfloat16 [4, 8192, 10240], P('section', None, 'tensor'), may hold values from -1 to 1
- out_proj: bfloat16 [4, 10240, 8192], P('section', 'tensor'), may hold values from -0.0625 to 0.0625
Outputs:
- section_grads: bfloat16 [4, 2, 64, 8192], P('section')
- gain_grads: float32 [4, 8192], P('section')
- conv_grads: float32 [4, 4, 10240], P('section', None, 'tensor')
The draws below stay inside these ranges and needn't reach their ends.
Inputs may be any that keep to these rules, and one draw needn't show every extreme that they name: `counts`: one micro-batch holds all 64 positions; the other holds 8 to 32 tokens.
All inputs are finite; a program needn't handle non-finite values.
Results may differ from the reference program's by a relative error of at most 0.033.
Values may be sent and summed in bfloat16 or wider, within the bound.
No kernel may reach another device: no remote copies, remote signals or barrier semaphores. Data moves between devices by JAX's collectives and lax.ppermute only.
A program may use at most 128 MiB of HBM per device.

```python
import math
import jax
import jax.numpy as jnp
from jax import lax

D = 8192
CH = 10240
KW = 4
MB = 2
SEQ = 64
N_SECTION = 4
N_TENSOR = 8


def draw_counts(key, part):
    key_short, key_full = jax.random.split(jax.random.fold_in(key, 11))
    short_len = jax.random.randint(key_short, (), SEQ // 8, SEQ // 2 + 1)
    full_slot = jax.random.randint(key_full, (), 0, MB)
    return jnp.where(jnp.arange(MB) == full_slot, SEQ, short_len).astype(jnp.int32)


def draw_layer_in(key, part):
    key_rows, key_cols, key_base, key_common = jax.random.split(jax.random.fold_in(key, 23), 4)
    row_scale = jnp.exp(jax.random.uniform(key_rows, (N_SECTION, MB, SEQ, 1), minval=math.log(0.1), maxval=0.0))
    col_scale = jnp.exp(jax.random.uniform(key_cols, (N_SECTION, 1, 1, D), minval=0.0, maxval=math.log(10.0)))
    base_vals = jnp.clip(jax.random.normal(key_base, (N_SECTION, MB, SEQ, D)), -4.0, 4.0)
    base_vals = base_vals + jnp.clip(jax.random.normal(key_common, (N_SECTION, MB, SEQ, 1)), -2.0, 2.0)
    return (base_vals * row_scale * col_scale).astype(jnp.bfloat16)


def draw_in_proj(key, part):
    key_base, key_offset = jax.random.split(jax.random.fold_in(key, 37))
    weight_scale = 1.0 / math.sqrt(D)
    base_vals = jnp.clip(jax.random.normal(key_base, (N_SECTION, D, CH)), -4.0, 4.0)
    offset_vals = 0.7 * jnp.clip(jax.random.normal(key_offset, (N_SECTION, 1, CH)), -3.0, 3.0)
    return ((base_vals + offset_vals) * weight_scale).astype(jnp.bfloat16)


def place_ends(entries, key, least, high):
    shape = entries.shape
    place = [jax.random.randint(jax.random.fold_in(key, axis), (), 0, shape[axis]) for axis in range(len(shape))]
    entries = entries.at[tuple(place)].set(least)
    longest = shape.index(max(shape))
    place[longest] = (place[longest] + 1) % shape[longest]
    return entries.at[tuple(place)].set(high)


def block_scale(own_key, shape, cuts, smallest, largest):
    def one(dim, shards_of):
        heights = jax.random.uniform(jax.random.fold_in(jax.random.fold_in(own_key, 6), dim), (shards_of,), jnp.float32, smallest / len(cuts), largest / len(cuts))
        return jnp.repeat(jnp.exp(heights), shape[dim] // shards_of).reshape((-1,) + (1,) * (len(shape) - dim - 1))

    level = one(*cuts[0])
    for cut in cuts[1:]:
        level = level * one(*cut)
    return level


def gaussian(key, extent, width, most, cuts=(), held_as=jnp.bfloat16):
    result = jax.random.normal(key, extent, jnp.float32) * width
    if len(cuts) > 0:
        result = block_scale(key, extent, cuts, -0.22, 0.18) * result
    return jnp.clip(result, min=-most, max=most).astype(held_as)


def setup_inputs(seed: int = 0) -> dict:
    splits = jax.random.split(jax.random.key(seed), 10)
    dy_top = gaussian(splits[0], (MB, SEQ, D), 1.0, 6.0)
    loss_mask = place_ends((jax.random.randint(splits[1], (MB, SEQ), 0, 4) < 3).astype(jnp.int32), jax.random.fold_in(splits[1], 1), 0, 1)
    counts = draw_counts(jax.random.fold_in(splits[9], 71), 0)
    layer_in = draw_layer_in(jax.random.fold_in(splits[9], 71), 0)
    conv_in = gaussian(splits[4], (N_SECTION, MB, SEQ, CH), 1.0, 6.0, ((0, 4), (3, 8)))
    norm_gain = jnp.clip(jnp.exp(math.log(3.0) - 2.3025851 * jax.random.uniform(splits[5], (N_SECTION, D), jnp.float32) ** block_scale(splits[5], (N_SECTION, D), ((0, 4),), -0.2, 0.2)), 0.3, 3.0)
    conv_weight = gaussian(splits[6], (N_SECTION, KW, CH), 0.5, 2.5, ((0, 4), (2, 8)), jnp.float32)
    in_proj = draw_in_proj(jax.random.fold_in(splits[9], 71), 0)
    out_proj = gaussian(splits[8], (N_SECTION, CH, D), CH ** -0.5, 0.0625, ((0, 4), (1, 8)))
    return {"dy_top": dy_top, "loss_mask": loss_mask, "counts": counts, "layer_in": layer_in, "conv_in": conv_in, "norm_gain": norm_gain, "conv_weight": conv_weight, "in_proj": in_proj, "out_proj": out_proj}


EPSILON = 1e-05

def conv_backward(weights, values, d_act):
    kernel_width = weights.shape[0]
    length = values.shape[0]
    padded = jnp.pad(values, ((kernel_width - 1, 0), (0, 0)))
    pre_act = jnp.zeros_like(values)
    for lag_idx in range(kernel_width):
        pre_act = pre_act + weights[lag_idx] * padded[kernel_width - 1 - lag_idx:kernel_width - 1 - lag_idx + length]
    gate_sig = jax.nn.sigmoid(pre_act)
    d_pre = d_act * gate_sig * (1.0 + pre_act * (1.0 - gate_sig))
    padded_back = jnp.pad(d_pre, ((0, kernel_width - 1), (0, 0)))
    d_vals = jnp.zeros_like(d_pre)
    for lag_idx in range(kernel_width):
        d_vals = d_vals + weights[lag_idx] * padded_back[lag_idx:lag_idx + length]
    lag_grads = jnp.stack([lax.optimization_barrier(jnp.sum(d_pre * padded[kernel_width - 1 - lag_idx:kernel_width - 1 - lag_idx + length], axis=0)) for lag_idx in range(kernel_width)])
    return (d_vals.astype(jnp.bfloat16), lag_grads)

def norm_backward(d_norm, saved_now, upstream, gain_vec):
    values = saved_now.astype(jnp.float32)
    inv_rms = lax.rsqrt(lax.optimization_barrier(jnp.mean(values * values, axis=-1, keepdims=True)) + EPSILON)
    normed = values * inv_rms
    d_hat = d_norm * gain_vec
    d_in = inv_rms * (d_hat - normed * lax.optimization_barrier(jnp.mean(d_hat * normed, axis=-1, keepdims=True)))
    return (upstream.astype(jnp.float32) + d_in, lax.optimization_barrier(jnp.sum(d_norm * normed, axis=0)))

def reference(dy_top, loss_mask, counts, layer_in, conv_in, norm_gain, conv_weight, in_proj, out_proj):
    positions = jnp.arange(SEQ, dtype=jnp.int32)
    keep_mask = (loss_mask == 1) & (positions[None, :] < counts[:, None])
    grad_now = jnp.where(keep_mask[:, :, None], dy_top, jnp.zeros_like(dy_top))
    block_size = CH // N_TENSOR
    section_list = []
    gain_list = []
    conv_list = []
    for section_idx in reversed(range(N_SECTION)):
        d_act = jnp.einsum('msd,cd->msc', grad_now.astype(jnp.float32), out_proj[section_idx].astype(jnp.float32))
        d_vals, lag_grads = jax.vmap(conv_backward, in_axes=(None, 0, 0))(conv_weight[section_idx], conv_in[section_idx].astype(jnp.float32), d_act)
        conv_grad = lax.optimization_barrier(jnp.sum(lag_grads, axis=0))
        d_norm = jnp.zeros((MB, SEQ, D), jnp.float32)
        for part_idx in range(N_TENSOR):
            first = part_idx * block_size
            term = jnp.einsum('msc,dc->msd', d_vals[:, :, first:first + block_size].astype(jnp.float32), in_proj[section_idx][:, first:first + block_size].astype(jnp.float32))
            rounded = lax.optimization_barrier(term.astype(jnp.bfloat16))
            d_norm = d_norm + rounded.astype(jnp.float32)
        grad_next, gain_grad = norm_backward(d_norm.reshape(MB * SEQ, D), layer_in[section_idx].reshape(MB * SEQ, D), grad_now.reshape(MB * SEQ, D), norm_gain[section_idx])
        grad_now = grad_next.astype(jnp.bfloat16).reshape(MB, SEQ, D)
        section_list.append(grad_now)
        gain_list.append(gain_grad)
        conv_list.append(conv_grad)
    section_list = section_list[::-1]
    gain_list = gain_list[::-1]
    conv_list = conv_list[::-1]
    return (jnp.stack(section_list), jnp.stack(gain_list), jnp.stack(conv_list))
```

```python
import functools

import jax
import jax.numpy as jnp
from jax import lax
from jax.experimental import pallas as pl
from jax.experimental.pallas import tpu as pltpu
from jax.sharding import PartitionSpec as P

EPSILON = 1e-05
QUARTERS = 4
F32 = jnp.float32
BF16 = jnp.bfloat16
NT = (((1,), (1,)), ((), ()))
VMEM = pl.BlockSpec(memory_space=pltpu.VMEM)
SMEM = pl.BlockSpec(memory_space=pltpu.SMEM)
MIB = 1 << 20


def kernel_call(body, out_shape, operands, scratch=(), limit=14, flops=0, moved=0):
    specs = [SMEM if op.dtype == jnp.int32 else VMEM for op in operands]
    return pl.pallas_call(
        body,
        in_specs=specs,
        out_specs=jax.tree.map(lambda _: VMEM, out_shape),
        out_shape=out_shape,
        scratch_shapes=list(scratch),
        compiler_params=pltpu.CompilerParams(vmem_limit_bytes=limit * MIB),
        cost_estimate=pl.CostEstimate(flops=flops, bytes_accessed=moved, transcendentals=0),
    )(*operands)


def resident(weights):
    return pltpu.with_memory_space_constraint(weights, pltpu.VMEM)


def conv_rows(d_act, slope, taps, segments):
    d_pre = d_act * slope
    rows = d_pre.shape[0]
    row = lax.broadcasted_iota(jnp.int32, d_pre.shape, 0)
    d_vals = taps[0:1] * d_pre
    for lag in range(1, taps.shape[0]):
        keep = row < rows - lag
        end = 0
        for length in segments[:-1]:
            end += length
            keep = keep & ((row < end - lag) | (row >= end))
        ahead = pltpu.roll(d_pre, rows - lag, 0)
        d_vals = d_vals + taps[lag : lag + 1] * jnp.where(keep, ahead, 0.0)
    return d_pre, d_vals


def act_kernel(segments, pieces, first, last, idx_ref, *refs):
    rows_refs, refs = refs[:pieces], refs[pieces:]
    w_ref, refs = refs[0], refs[1:]
    if not first:
        so_far, refs = refs[0], refs[1:]
    if last:
        slope_ref, taps_ref, refs = refs[0], refs[1], refs[2:]
        vals_ref, pre_ref, refs = refs[0], refs[1], refs[2:]
    else:
        out_ref, refs = refs[0], refs[1:]
    acc_ref, refs = refs[0], refs[1:]
    chunk = 512
    if pieces == 1:
        width = w_ref.shape[1]
        base = 0
    else:
        joined = refs[0]
        width = joined.shape[2]
        base = idx_ref[0] * width
        for piece in range(pieces):
            joined[idx_ref[1 + piece]] = rows_refs[piece][...].astype(F32)
    for at in range(0, width, chunk):
        if pieces == 1:
            left = rows_refs[0][:, at : at + chunk]
        else:
            left = joined[:, :, at : at + chunk].reshape(-1, chunk).astype(BF16)
        columns = pl.ds(pl.multiple_of(base + at, chunk), chunk)
        term = lax.dot_general(left, w_ref[:, columns], NT, preferred_element_type=F32)
        if at > 0:
            acc_ref[...] += term
        elif first:
            acc_ref[...] = term
        else:
            acc_ref[...] = so_far[...] + term
    if not last:
        out_ref[...] = acc_ref[...]
        return
    block = 256
    for at in range(0, acc_ref.shape[1], block):
        part = slice(at, at + block)
        d_pre, d_vals = conv_rows(acc_ref[:, part], slope_ref[:, part], taps_ref[:, part], segments)
        pre_ref[:, part] = d_pre
        vals_ref[:, part] = d_vals.astype(BF16)


def other_part_kernel(idx_ref, vals_ref, w_ref, out_ref):
    width = out_ref.shape[1]
    chunk = 512
    for at in range(0, width, chunk):
        features = pl.ds(pl.multiple_of(idx_ref[0] * width + at, chunk), chunk)
        out_ref[:, at : at + chunk] = lax.dot_general(
            vals_ref[...], w_ref[features, :], NT, preferred_element_type=F32
        ).astype(BF16)


def own_part_kernel(received, idx_ref, vals_ref, w_ref, *refs):
    recv_refs, (keep_ref, send_ref, cut_ref) = refs[:received], refs[received:]
    width = keep_ref.shape[2]
    block_rows = keep_ref.shape[1]
    chunk = 512
    for at in range(0, width, chunk):
        part = slice(at, at + chunk)
        features = pl.ds(pl.multiple_of(idx_ref[0] * width + at, chunk), chunk)
        term = lax.dot_general(
            vals_ref[...], w_ref[features, :], NT, preferred_element_type=F32
        )
        for recv in recv_refs:
            term = term + recv[:, part].astype(F32)
        cut_ref[:, :, part] = term.reshape(QUARTERS, block_rows, chunk)
    for slot in range(2):
        keep_ref[slot] = cut_ref[idx_ref[1 + slot]]
        send_ref[slot] = cut_ref[idx_ref[3 + slot]].astype(BF16)


def lane_sums(values):
    total = values[:, 0:128]
    for at in range(128, values.shape[1], 128):
        total = total + values[:, at : at + 128]
    return total


def norm_sums_kernel(keep_ref, first_ref, second_ref, normed_ref, gain_ref, d_ref, part_ref, gsum_ref):
    d_norm = keep_ref[0] + first_ref[0].astype(F32) + second_ref[...].astype(F32)
    d_ref[...] = d_norm
    product = d_norm * normed_ref[...]
    gsum_ref[...] = jnp.sum(product, axis=0, keepdims=True)
    part_ref[...] = lane_sums(product * gain_ref[...])


def norm_grad_kernel(features, parts, d_ref, normed_ref, gain_ref, inv_ref, up_ref, *refs):
    part_refs, (out_ref,) = refs[:parts], refs[parts:]
    total = part_refs[0][...]
    for ref in part_refs[1:]:
        total = total + ref[...]
    mean = jnp.sum(total, axis=1, keepdims=True) * (1.0 / features)
    d_hat = d_ref[...] * gain_ref[...]
    d_in = inv_ref[...] * (d_hat - normed_ref[...] * mean)
    out_ref[...] = (up_ref[...].astype(F32) + d_in).astype(BF16)


def assemble_kernel(parts, full_rows, idx_ref, *refs):
    pieces, (out_ref, cut_ref) = refs[: parts * QUARTERS], refs[parts * QUARTERS :]
    width = cut_ref.shape[2]
    rows = QUARTERS * cut_ref.shape[1]
    short_rows = rows - full_rows
    full = idx_ref[0]
    for part in range(parts):
        at = 1 + part * (QUARTERS + 1)
        for piece in range(QUARTERS):
            cut_ref[idx_ref[at + 1 + piece]] = pieces[part * QUARTERS + piece][...].astype(F32)
        columns = pl.ds(pl.multiple_of(idx_ref[at] * width, width), width)
        whole = cut_ref[...].reshape(rows, width).astype(BF16)
        out_ref[full, :, columns] = whole[:full_rows]
        out_ref[1 - full, :short_rows, columns] = whole[full_rows:]
        out_ref[1 - full, short_rows:, columns] = jnp.zeros((full_rows - short_rows, width), BF16)


def local(dy_top, loss_mask, counts, layer_in, conv_in, norm_gain, conv_weight, in_proj, out_proj):
    sections = lax.axis_size("section")
    tensors = lax.axis_size("tensor")
    section = lax.axis_index("section")
    me = lax.axis_index("tensor")
    seq = dy_top.shape[1]
    model = dy_top.shape[2]
    short = seq // 2
    rows = seq + short
    block_rows = rows // QUARTERS
    parts = tensors // QUARTERS
    width = model // parts
    w_in, w_out, taps = in_proj[0], out_proj[0], conv_weight[0]
    lags, channels = taps.shape

    full = jnp.where(counts[0] == seq, 0, 1).astype(jnp.int32)

    def live(array):
        head = lax.dynamic_index_in_dim(array, full, 0, keepdims=False)
        tail = lax.dynamic_index_in_dim(array, 1 - full, 0, keepdims=False)[:short]
        return jnp.concatenate([head, tail], axis=0)

    near, far = parts, 2 * parts
    odd = lax.rem(me, 2)
    quarter = 2 * jnp.where((me & near) != 0, 1, 0) + jnp.where((me & far) != 0, 1, 0)
    own_part = lax.rem(me, parts)

    def places(is_odd):
        first, second = 2 - is_odd, 1 + is_odd
        return [quarter, quarter ^ second, quarter ^ first, quarter ^ 3]

    def packed(values):
        return jnp.stack([jnp.asarray(v, jnp.int32) for v in values])

    mine = packed([own_part] + places(odd))
    others = []
    for distance in range(1, parts):
        side = odd ^ (distance & 1)
        others.append(packed([own_part ^ distance] + places(side)))

    def swapped(x, axis_bits):
        return lax.ppermute(x, "tensor", [(i, i ^ axis_bits(i)) for i in range(tensors)])

    def first_hop(x):
        return swapped(x, lambda i: near if i % 2 == 0 else far)

    def second_hop(x):
        return swapped(x, lambda i: far if i % 2 == 0 else near)

    def sideways(x, distance):
        return swapped(x, lambda i: distance)

    def below(x):
        return lax.ppermute(x, "section", [(i, i - 1) for i in range(1, sections)])

    def gathered(own):
        second = second_hop(own)
        third = first_hop(own)
        fourth = first_hop(second)
        pieces = [own, second, third, fourth]
        return [pieces] + [[sideways(p, d) for p in pieces] for d in range(1, parts)]

    positions = jnp.arange(seq, dtype=jnp.int32)
    keep_mask = (loss_mask == 1) & (positions[None, :] < counts[:, None])
    top = live(jnp.where(keep_mask[:, :, None], dy_top, jnp.zeros_like(dy_top)))

    def shifted(values, lag):
        moved = jnp.pad(values, ((lag, 0), (0, 0)))[: values.shape[0]]
        row = jnp.arange(rows)[:, None]
        return jnp.where((row >= seq) & (row < seq + lag), 0.0, moved)

    conv_live = live(conv_in[0]).astype(F32)
    lagged = [shifted(conv_live, lag) for lag in range(lags)]
    pre_act = functools.reduce(jnp.add, [taps[k] * lagged[k] for k in range(lags)])
    gate = jax.nn.sigmoid(pre_act)
    slope = gate * (1.0 + pre_act * (1.0 - gate))

    def own_block(array):
        return lax.dynamic_slice(
            array, (quarter * block_rows, own_part * width), (block_rows, width)
        )

    layer_live = live(layer_in[0])
    layer_rows = lax.dynamic_slice(
        layer_live, (quarter * block_rows, 0), (block_rows, model)
    ).astype(F32)
    inv_rms = lax.rsqrt(jnp.mean(layer_rows * layer_rows, axis=-1, keepdims=True) + EPSILON)
    normed = (
        lax.dynamic_slice(layer_rows, (0, own_part * width), (block_rows, width)) * inv_rms
    )
    gain = lax.dynamic_slice(norm_gain, (0, own_part * width), (1, width))

    sds = jax.ShapeDtypeStruct
    joined = pltpu.VMEM((QUARTERS, block_rows, width), F32)
    matmul_cost = dict(flops=2 * rows * channels * width, moved=2 * channels * width)

    def activation(step, incoming):
        ends = (sds((rows, channels), BF16), sds((rows, channels), F32))
        acc = pltpu.VMEM((rows, channels), F32)
        if step == 0:
            body = functools.partial(act_kernel, (seq, short), 1, True, True)
            return kernel_call(
                body, ends, [mine, top, resident(w_out), slope, taps], [acc], 18, **matmul_cost
            )
        groups = gathered(incoming)
        total = None
        for number, group in enumerate(groups):
            first, last = number == 0, number == parts - 1
            body = functools.partial(act_kernel, (seq, short), QUARTERS, first, last)
            operands = [mine if number == 0 else others[number - 1]] + group + [resident(w_out)]
            operands += [] if first else [total]
            operands += [slope, taps] if last else []
            total = kernel_call(
                body,
                ends if last else sds((rows, channels), F32),
                operands,
                [acc, joined],
                18,
                **matmul_cost,
            )
        return total

    def summed(d_vals):
        received = []
        for distance in range(1, parts):
            partial = kernel_call(
                other_part_kernel,
                sds((rows, width), BF16),
                [others[distance - 1], d_vals, resident(w_in)],
                **matmul_cost,
            )
            received.append(sideways(partial, distance))
        keep, send = kernel_call(
            functools.partial(own_part_kernel, len(received)),
            (sds((2, block_rows, width), F32), sds((2, block_rows, width), BF16)),
            [mine, d_vals, resident(w_in)] + received,
            [joined],
            18,
            **matmul_cost,
        )
        first = first_hop(send)
        passed = (keep[1] + first[1].astype(F32)).astype(BF16)
        return keep, first, second_hop(passed)

    upstream = own_block(top)
    own_grad = jnp.zeros((block_rows, width), BF16)
    own_gain = jnp.zeros((1, width), F32)
    own_pre = jnp.zeros((rows, channels), F32)
    for step in range(sections):
        active = section == sections - 1 - step
        d_vals, d_pre = activation(step, upstream)
        keep, first, second = summed(d_vals)
        d_norm, part, gain_sum = kernel_call(
            norm_sums_kernel,
            (sds((block_rows, width), F32), sds((block_rows, 128), F32), sds((1, width), F32)),
            [keep, first, second, normed, gain],
        )
        shares = [part] + [sideways(part, d) for d in range(1, parts)]
        grad = kernel_call(
            functools.partial(norm_grad_kernel, model, parts),
            sds((block_rows, width), BF16),
            [d_norm, normed, gain, inv_rms, upstream] + shares,
        )
        own_grad = jnp.where(active, grad, own_grad)
        own_gain = jnp.where(active, gain_sum, own_gain)
        own_pre = jnp.where(active, d_pre, own_pre)
        if step < sections - 1:
            upstream = below(grad)

    groups = gathered(own_grad)
    where = [full[None], mine] + others
    result = kernel_call(
        functools.partial(assemble_kernel, parts, seq),
        sds((2, seq, model), BF16),
        [jnp.concatenate(where)] + [piece for group in groups for piece in group],
        [joined],
        18,
    )
    conv_grads = jnp.stack([jnp.sum(own_pre * lagged[k], axis=0) for k in range(lags)])
    gain_rows = own_gain + first_hop(own_gain)
    gain_rows = gain_rows + second_hop(gain_rows)
    gain_parts = [gain_rows] + [sideways(gain_rows, d) for d in range(1, parts)]
    gain_total = jnp.concatenate(
        [
            functools.reduce(
                lambda a, b: jnp.where((own_part ^ part) == b[0], b[1], a),
                list(enumerate(gain_parts))[1:],
                gain_parts[0],
            )
            for part in range(parts)
        ],
        axis=1,
    )
    return (result[None], gain_total, conv_grads[None])


def solution(mesh):
    placed = (
        P(),
        P(),
        P(),
        P("section", None, None, None),
        P("section", None, None, "tensor"),
        P("section", None),
        P("section", None, "tensor"),
        P("section", None, "tensor"),
        P("section", "tensor", None),
    )
    return jax.shard_map(
        local,
        mesh=mesh,
        in_specs=placed,
        out_specs=(
            P("section", None, None, None),
            P("section", None),
            P("section", None, "tensor"),
        ),
        check_vma=False,
    )
```

```python
import functools

import jax
import jax.numpy as jnp
from jax import lax
from jax.experimental import pallas as pl
from jax.experimental.pallas import tpu as pltpu
from jax.sharding import PartitionSpec as P

EPSILON = 1e-05
CHIPS = 4
LANES = 128
GAIN_ROWS = 8
F32 = jnp.float32
BF16 = jnp.bfloat16
NT = (((1,), (1,)), ((), ()))
NN = (((1,), (0,)), ((), ()))
VMEM = pl.BlockSpec(memory_space=pltpu.VMEM)
SMEM = pl.BlockSpec(memory_space=pltpu.SMEM)
HBM = pl.BlockSpec(memory_space=pltpu.HBM)
MIB = 1 << 20
SDS = jax.ShapeDtypeStruct


def kernel_call(body, out_shape, operands, scratch=(), limit=4, flops=0, moved=0, specs=None):
    specs = specs or [SMEM if op.dtype == jnp.int32 else VMEM for op in operands]
    return pl.pallas_call(
        body,
        in_specs=specs,
        out_specs=jax.tree.map(lambda _: VMEM, out_shape, is_leaf=lambda s: hasattr(s, "shape")),
        out_shape=out_shape,
        scratch_shapes=list(scratch),
        compiler_params=pltpu.CompilerParams(vmem_limit_bytes=limit * MIB),
        cost_estimate=pl.CostEstimate(flops=flops, bytes_accessed=moved, transcendentals=0),
    )(*operands)


def resident(weights):
    return pltpu.with_memory_space_constraint(weights, pltpu.VMEM)


def moved_rows(values, by, seq):
    rows = values.shape[0]
    row = lax.broadcasted_iota(jnp.int32, values.shape, 0)
    if by > 0:
        keep = (row >= by) & ((row < seq) | (row >= seq + by))
        turned = pltpu.roll(values, by, 0)
    else:
        keep = (row < rows + by) & ((row < seq + by) | (row >= seq))
        turned = pltpu.roll(values, rows + by, 0)
    return jnp.where(keep, turned, 0.0)


def conv_backward(
    seq, acc_ref, slope_ref, rows_ref, taps_ref, inner_ref, vals_ref, grads_ref, active=None, kept_ref=None
):
    rows, channels = acc_ref.shape
    lags = taps_ref.shape[0]
    block = 256 if channels % 256 == 0 else LANES
    sums = jnp.zeros((rows, LANES), F32)

    def set_grads(lag, part, value):
        row = slice(lag, lag + 1)
        if kept_ref is not None:
            value = jnp.where(active, value, kept_ref[row, part])
        grads_ref[row, part] = value

    for at in range(0, channels, block):
        part = slice(at, at + block)
        d_pre = acc_ref[:, part] * slope_ref[:, part]
        values = rows_ref[:, part]
        d_vals = taps_ref[0:1, part] * d_pre
        set_grads(0, part, jnp.sum(d_pre * values, axis=0, keepdims=True))
        for lag in range(1, lags):
            ahead = moved_rows(d_pre, -lag, seq)
            d_vals = d_vals + taps_ref[lag : lag + 1, part] * ahead
            set_grads(lag, part, jnp.sum(ahead * values, axis=0, keepdims=True))
        rounded = d_vals.astype(BF16)
        vals_ref[:, part] = rounded
        product = rounded.astype(F32) * inner_ref[:, part]
        for lane in range(0, block, LANES):
            sums = sums + product[:, lane : lane + LANES]
    return jnp.broadcast_to(jnp.sum(sums, axis=1, keepdims=True), (rows, LANES))


def first_kernel(
    seq,
    me_slot,
    idx_ref,
    keep_ref,
    dy_ref,
    layer_ref,
    conv_ref,
    gain_ref,
    taps_ref,
    wo_hbm,
    wi_hbm,
    *refs,
):
    vals_ref, grads_ref, sums_ref, inner_ref, slope_ref, rows_ref, *refs = refs
    normed_ref, inv_ref, up_ref, *refs = refs
    *weights, top_ref, acc_ref, sem = refs
    blocks = len(weights) // 2
    wo_refs, wi_refs = weights[:blocks], weights[blocks:]
    full = idx_ref[0]
    model = gain_ref.shape[1]
    width = up_ref.shape[1]
    channels = taps_ref.shape[1]
    lags = taps_ref.shape[0]
    short = acc_ref.shape[0] - seq
    copies = []
    for i in range(blocks):
        columns = pl.ds(pl.multiple_of(idx_ref[me_slot + i] * width, width), width)
        copies.append(pltpu.make_async_copy(wo_hbm.at[:, columns], wo_refs[i], sem.at[i]))
    for i in range(blocks):
        features = pl.ds(pl.multiple_of(idx_ref[me_slot + i] * width, width), width)
        copies.append(pltpu.make_async_copy(wi_hbm.at[features, :], wi_refs[i], sem.at[blocks + i]))
    for copy in copies:
        copy.start()

    def live(ref, part):
        head = ref[full, :, part].astype(F32)
        tail = ref[1 - full, :short, part].astype(F32)
        return jnp.concatenate([head, tail], axis=0)

    keep = keep_ref[:, 0:1]
    squares = jnp.zeros((seq + short, LANES), F32)
    chunk = min(1024, width)
    for i in range(model // chunk):
        part = slice(i * chunk, (i + 1) * chunk)
        top_ref[:, part] = (live(dy_ref, part) * keep).astype(BF16)
        values = live(layer_ref, part)
        values = values * values
        for lane in range(0, chunk, LANES):
            squares = squares + values[:, lane : lane + LANES]
    mean = jnp.sum(squares, axis=1, keepdims=True) * (1.0 / model)
    inv = lax.rsqrt(mean + EPSILON)
    inv_ref[...] = jnp.broadcast_to(inv, inv_ref.shape)
    mine = pl.ds(pl.multiple_of(idx_ref[me_slot] * width, width), width)
    normed_ref[...] = live(layer_ref, mine) * inv
    up_ref[...] = top_ref[:, mine]
    block = 256 if channels % 256 == 0 else LANES
    for at in range(0, channels, block):
        part = slice(at, at + block)
        values = live(conv_ref, part)
        rows_ref[:, part] = values
        pre_act = taps_ref[0:1, part] * values
        for lag in range(1, lags):
            pre_act = pre_act + taps_ref[lag : lag + 1, part] * moved_rows(values, lag, seq)
        gate = 1.0 / (1.0 + jnp.exp(-pre_act))
        slope_ref[:, part] = gate * (1.0 + pre_act * (1.0 - gate))

    half = min(512, width)
    for i in range(blocks):
        copies[i].wait()
        for at in range(0, width, half):
            part = pl.ds(pl.multiple_of(idx_ref[me_slot + i] * width + at, half), half)
            term = lax.dot_general(
                top_ref[:, part], wo_refs[i][:, at : at + half], NT, preferred_element_type=F32
            )
            if i + at == 0:
                acc_ref[...] = term
            else:
                acc_ref[...] += term
    for i in range(blocks):
        copies[blocks + i].wait()
        for at in range(0, width, half):
            part = pl.ds(pl.multiple_of(idx_ref[me_slot + i] * width + at, half), half)
            scaled = (live(layer_ref, part) * inv * gain_ref[:, part]).astype(BF16)
            term = lax.dot_general(
                scaled, wi_refs[i][at : at + half, :], NN, preferred_element_type=F32
            )
            if i + at == 0:
                inner_ref[...] = term
            else:
                inner_ref[...] += term
    sums_ref[...] = conv_backward(
        seq, acc_ref, slope_ref, rows_ref, taps_ref, inner_ref, vals_ref, grads_ref
    )


def act_kernel(seq, count, flag, first, last, idx_ref, *refs):
    pieces, wo_refs, refs = refs[:count], refs[count : 2 * count], refs[2 * count :]
    if not first:
        so_far, refs = refs[0], refs[1:]
    if last:
        slope_ref, rows_ref, taps_ref, inner_ref, kept_ref, vals_ref, grads_ref, sums_ref, acc_ref = refs
    else:
        (acc_ref,) = refs
    width = pieces[0].shape[1]
    chunk = min(512, width)
    base = None if first else so_far
    for piece, wo_ref in zip(pieces, wo_refs):
        for at in range(0, width, chunk):
            part = slice(at, at + chunk)
            term = lax.dot_general(
                piece[:, part], wo_ref[:, part], NT, preferred_element_type=F32
            )
            acc_ref[...] = term if base is None else base[...] + term
            base = acc_ref
    if last:
        active = idx_ref[flag] == 1
        sums_ref[...] = conv_backward(
            seq, acc_ref, slope_ref, rows_ref, taps_ref, inner_ref, vals_ref, grads_ref, active, kept_ref
        )


def block_product(vals_ref, wi_ref, at, chunk):
    return lax.dot_general(
        vals_ref[...], wi_ref[at : at + chunk, :], NT, preferred_element_type=F32
    )


def split_sums(sums):
    high = sums.astype(BF16)
    low = (sums - high.astype(F32)).astype(BF16)
    lane = lax.broadcasted_iota(jnp.int32, sums.shape, 1)
    return jnp.where(lane < LANES // 2, high.astype(F32), low.astype(F32)).astype(BF16)


def joined_sums(block, width):
    high = block[:, width : width + 1].astype(F32)
    return high + block[:, width + LANES // 2 : width + LANES // 2 + 1].astype(F32)


def other_blocks_kernel(vals_ref, sums_ref, *refs):
    wi_refs, out_ref = refs[:-1], refs[-1]
    width = out_ref.shape[2] - LANES
    chunk = min(512, width)
    for number, wi_ref in enumerate(wi_refs):
        for at in range(0, width, chunk):
            term = block_product(vals_ref, wi_ref, at, chunk)
            out_ref[number, :, at : at + chunk] = term.astype(BF16)
        out_ref[number, :, width:] = split_sums(sums_ref[...])


def own_blocks_kernel(chips, vals_ref, sums_ref, *refs):
    count = len(chips)
    wi_refs, recv_refs, out_refs = refs[:count], refs[count:-count], refs[-count:]
    width = out_refs[0].shape[1] - LANES
    chunk = min(512, width)
    for number, (chip, wi_ref, out_ref) in enumerate(zip(chips, wi_refs, out_refs)):
        for at in range(0, width, chunk):
            term = block_product(vals_ref, wi_ref, at, chunk)
            for recv in recv_refs:
                term = term + recv[number, :, at : at + chunk].astype(F32)
            out_ref[:, at : at + chunk] = term.astype(out_ref.dtype)
        sums = sums_ref[...]
        for recv in recv_refs:
            sums = sums + joined_sums(recv[number], width)
        out_ref[:, width:] = split_sums(sums) if chip else sums


def norm_kernel(
    model,
    me_slot,
    flag,
    first,
    last,
    idx_ref,
    own_ref,
    a_ref,
    b_ref,
    c_ref,
    normed_ref,
    inv_ref,
    gain_ref,
    up_ref,
    *refs,
):
    if not first:
        earlier_ref, gains_ref, refs = refs[0], refs[1], refs[2:]
    if last:
        (out_ref,) = refs
    else:
        out_ref, kept_ref, sum_ref = refs
    rows, width = normed_ref.shape
    sums = own_ref[:, width : width + 1]
    for ref in (a_ref, b_ref, c_ref):
        sums = sums + joined_sums(ref, width)
    mean = sums * (1.0 / model)
    inv = inv_ref[:, 0:1]
    active = idx_ref[flag] == 1
    chunk = min(512, width)
    for at in range(0, width, chunk):
        part = slice(at, at + chunk)
        d_norm = own_ref[:, part]
        for ref in (a_ref, b_ref, c_ref):
            d_norm = d_norm + ref[:, part].astype(F32)
        normed = normed_ref[:, part]
        gain = gain_ref[:, pl.ds(pl.multiple_of(idx_ref[me_slot] * width + at, chunk), chunk)]
        d_in = inv * (d_norm * gain - normed * mean)
        grad = up_ref[:, part].astype(F32) + d_in
        gains = jnp.sum(d_norm * normed, axis=0, keepdims=True)
        kept = grad
        if not first:
            kept = jnp.where(active, grad, earlier_ref[:, part].astype(F32))
            gains = jnp.where(active, gains, gains_ref[:, part])
        if last:
            high = gains.astype(BF16).astype(F32)
            row = lax.broadcasted_iota(jnp.int32, (GAIN_ROWS, chunk), 0)
            both = jnp.where(row == 0, high, jnp.where(row == 1, gains - high, 0.0))
            out_ref[:rows, part] = kept.astype(BF16)
            out_ref[rows:, part] = both.astype(BF16)
        else:
            out_ref[:, part] = grad.astype(BF16)
            kept_ref[:, part] = kept.astype(BF16)
            sum_ref[:, part] = gains


def assemble_kernel(seq, rows, me_slot, idx_ref, *refs):
    pieces, (out_ref, gain_ref) = refs[:-2], refs[-2:]
    width = pieces[0].shape[1]
    full = idx_ref[0]
    short = rows - seq
    for number, piece in enumerate(pieces):
        columns = pl.ds(pl.multiple_of(idx_ref[me_slot + number] * width, width), width)
        out_ref[full, :, columns] = piece[:seq]
        out_ref[1 - full, :short, columns] = piece[seq:rows]
        out_ref[1 - full, short:, columns] = jnp.zeros((seq - short, width), BF16)
        gains = piece[rows:].astype(F32)
        gain_ref[:, columns] = gains[0:1] + gains[1:2]


def local(dy_top, loss_mask, counts, layer_in, conv_in, norm_gain, conv_weight, in_proj, out_proj):
    sections = lax.axis_size("section")
    tensors = lax.axis_size("tensor")
    section = lax.axis_index("section").astype(jnp.int32)
    me = lax.axis_index("tensor").astype(jnp.int32)
    seq, model = dy_top.shape[1:]
    short = seq // 2
    rows = seq + short
    parts = tensors // CHIPS
    width = model // tensors
    w_in, w_out, taps = in_proj[0], out_proj[0], conv_weight[0]
    lags, channels = taps.shape

    full = jnp.where(counts[0] == seq, 0, 1).astype(jnp.int32)
    positions = jnp.arange(seq, dtype=jnp.int32)
    keep = ((loss_mask == 1) & (positions[None, :] < counts[:, None])).astype(F32)
    keep_full = jnp.where(full == 0, keep[0], keep[1])
    keep_short = jnp.where(full == 0, keep[1], keep[0])[:short]
    keep_rows = jnp.broadcast_to(
        jnp.concatenate([keep_full, keep_short])[:, None], (rows, LANES)
    )

    me_slot = 1 + sections

    blocks = jnp.arange(tensors, dtype=jnp.int32) ^ me
    working = (jnp.arange(sections) == sections - 1 - section).astype(jnp.int32)
    table = jnp.concatenate([full[None], working, blocks])

    def across(x, chip):
        return lax.ppermute(x, "tensor", [(i, i ^ (chip * parts)) for i in range(tensors)])

    def sideways(x, side):
        return lax.ppermute(x, "tensor", [(i, i ^ side) for i in range(tensors)])

    def below(x):
        return lax.ppermute(x, "section", [(i, i - 1) for i in range(1, sections)])

    sides = range(1, parts)
    order = (3, 1, 2)
    product_cost = dict(flops=2 * rows * channels * width, moved=2 * channels * width)

    vals_shape = SDS((rows, channels), BF16)
    grads_shape = SDS((lags, channels), F32)
    sums_shape = SDS((rows, LANES), F32)
    channel_shape = SDS((rows, channels), F32)
    block_rows = [(channels, width)] * tensors + [(width, channels)] * tensors
    d_vals, tap_grads, sums, inner, slope, conv_rows, normed, inv, upstream, *weights = kernel_call(
        functools.partial(first_kernel, seq, me_slot),
        (
            vals_shape,
            grads_shape,
            sums_shape,
            channel_shape,
            channel_shape,
            channel_shape,
            SDS((rows, width), F32),
            SDS((rows, LANES), F32),
            SDS((rows, width), BF16),
        )
        + tuple(pltpu.VMEM(shape, BF16) for shape in block_rows),
        [table, keep_rows, dy_top, layer_in[0], conv_in[0], norm_gain, taps, w_out, w_in],
        [
            pltpu.VMEM((rows, model), BF16),
            pltpu.VMEM((rows, channels), F32),
            pltpu.SemaphoreType.DMA((2 * tensors,)),
        ],
        limit=12,
        flops=4 * rows * channels * model,
        moved=4 * channels * model,
        specs=[SMEM] + [VMEM] * 6 + [HBM] * 2,
    )
    wo, wi = weights[:tensors], weights[tensors:]

    def activation(step, own, taps_kept):
        far = {chip: across(own, chip) for chip in order}
        far[0] = own
        plan = []
        waiting = []
        for chip in (0,) + order:
            plan.append(waiting + [(chip, 0)])
            waiting = [(chip, side) for side in sides]
        plan.append(waiting)
        pieces = {(chip, 0): far[chip] for chip in far}
        for chip in far:
            for side in sides:
                pieces[chip, side] = sideways(far[chip], side)
        total = None
        for number, group in enumerate(plan):
            first, last = number == 0, number == len(plan) - 1
            operands = [table] + [pieces[key] for key in group]
            operands += [resident(wo[chip * parts + side]) for chip, side in group]
            operands += [] if first else [total]
            operands += [slope, conv_rows, taps, inner, taps_kept] if last else []
            total = kernel_call(
                functools.partial(
                    act_kernel, seq, len(group), 1 + step, first, last
                ),
                (vals_shape, grads_shape, sums_shape) if last else channel_shape,
                operands,
                [pltpu.VMEM((rows, channels), F32)] if last else [],
                flops=len(group) * product_cost["flops"],
                moved=len(group) * product_cost["moved"],
            )
        return total

    def summed(vals, row_sums):
        groups = (order[:2], (order[2], 0))
        received = []
        for chips in groups:
            received.append(
                [
                    sideways(
                        kernel_call(
                            other_blocks_kernel,
                            SDS((len(chips), rows, width + LANES), BF16),
                            [vals, row_sums]
                            + [resident(wi[chip * parts + side]) for chip in chips],
                            flops=2 * product_cost["flops"],
                            moved=2 * product_cost["moved"],
                        ),
                        side,
                    )
                    for side in sides
                ]
            )
        terms = {}
        for chips, others in zip(groups, received):
            blocks_out = kernel_call(
                functools.partial(own_blocks_kernel, chips),
                tuple(SDS((rows, width + LANES), BF16 if chip else F32) for chip in chips),
                [vals, row_sums] + [resident(wi[chip * parts]) for chip in chips] + others,
                flops=2 * product_cost["flops"],
                moved=2 * product_cost["moved"],
            )
            for chip, block in zip(chips, blocks_out):
                terms[chip] = across(block, chip) if chip else block
        return [terms[chip] for chip in (0,) + order]

    taps_kept = tap_grads
    for step in range(sections):
        first, last = step == 0, step == sections - 1
        if not first:
            d_vals, taps_kept, sums = activation(step, upstream, taps_kept)
        terms = summed(d_vals, sums)
        block = SDS((rows, width), BF16)
        results = kernel_call(
            functools.partial(norm_kernel, model, me_slot, 1 + step, first, last),
            SDS((rows + GAIN_ROWS, width), BF16) if last else (block, block, SDS((1, width), F32)),
            [table] + terms + [normed, inv, norm_gain, upstream] + ([] if first else [kept, gains]),
        )
        if last:
            own = results
        else:
            grad, kept, gains = results
            upstream = below(grad)

    far = [own] + [across(own, chip) for chip in range(1, CHIPS)]
    pieces = []
    for piece in far:
        pieces += [piece] + [sideways(piece, side) for side in sides]
    result, gain_grads = kernel_call(
        functools.partial(assemble_kernel, seq, rows, me_slot),
        (SDS((2, seq, model), BF16), SDS((1, model), F32)),
        [table] + pieces,
        limit=8,
    )
    return (result[None], gain_grads, taps_kept[None])


def solution(mesh):
    placed = (
        P(),
        P(),
        P(),
        P("section", None, None, None),
        P("section", None, None, "tensor"),
        P("section", None),
        P("section", None, "tensor"),
        P("section", None, "tensor"),
        P("section", "tensor", None),
    )
    return jax.shard_map(
        local,
        mesh=mesh,
        in_specs=placed,
        out_specs=(
            P("section", None, None, None),
            P("section", None),
            P("section", None, "tensor"),
        ),
        check_vma=False,
    )
```

```python
import functools

import jax
import jax.numpy as jnp
from jax import lax
from jax.experimental import pallas as pl
from jax.experimental.pallas import tpu as pltpu
from jax.sharding import PartitionSpec as P

EPSILON = 1e-05
CHIPS = 4
LANES = 128
GAIN_ROWS = 8
F32 = jnp.float32
BF16 = jnp.bfloat16
NT = (((1,), (1,)), ((), ()))
NN = (((1,), (0,)), ((), ()))
VMEM = pl.BlockSpec(memory_space=pltpu.VMEM)
SMEM = pl.BlockSpec(memory_space=pltpu.SMEM)
HBM = pl.BlockSpec(memory_space=pltpu.HBM)
ANY = pl.BlockSpec(memory_space=pl.ANY)
MIB = 1 << 20
SDS = jax.ShapeDtypeStruct


def kernel_call(
    body, out_shape, operands, scratch=(), limit=4, flops=0, moved=0, specs=None, after=None
):
    specs = specs or [SMEM if op.dtype == jnp.int32 else VMEM for op in operands]
    if after is not None:
        operands, specs = [after] + operands, [ANY] + specs
        body = functools.partial(skip_first, body)
    return pl.pallas_call(
        body,
        in_specs=specs,
        out_specs=jax.tree.map(lambda _: VMEM, out_shape, is_leaf=lambda s: hasattr(s, "shape")),
        out_shape=out_shape,
        scratch_shapes=list(scratch),
        compiler_params=pltpu.CompilerParams(vmem_limit_bytes=limit * MIB),
        cost_estimate=pl.CostEstimate(flops=flops, bytes_accessed=moved, transcendentals=0),
    )(*operands)


def skip_first(body, _, *refs):
    body(*refs)


def resident(weights):
    return pltpu.with_memory_space_constraint(weights, pltpu.VMEM)


def moved_rows(values, by, seq):
    rows = values.shape[0]
    row = lax.broadcasted_iota(jnp.int32, values.shape, 0)
    if by > 0:
        keep = (row >= by) & ((row < seq) | (row >= seq + by))
        turned = pltpu.roll(values, by, 0)
    else:
        keep = (row < rows + by) & ((row < seq + by) | (row >= seq))
        turned = pltpu.roll(values, rows + by, 0)
    return jnp.where(keep, turned, 0.0)


def conv_backward(
    seq, acc_ref, slope_ref, rows_ref, taps_ref, inner_ref, vals_ref, grads_ref, active=None, kept_ref=None
):
    rows, channels = acc_ref.shape
    lags = taps_ref.shape[0]
    block = 256 if channels % 256 == 0 else LANES
    sums = jnp.zeros((rows, LANES), F32)

    def set_grads(lag, part, value):
        row = slice(lag, lag + 1)
        if kept_ref is not None:
            value = jnp.where(active, value, kept_ref[row, part])
        grads_ref[row, part] = value

    for at in range(0, channels, block):
        part = slice(at, at + block)
        d_pre = acc_ref[:, part] * slope_ref[:, part]
        values = rows_ref[:, part]
        d_vals = taps_ref[0:1, part] * d_pre
        set_grads(0, part, jnp.sum(d_pre * values, axis=0, keepdims=True))
        for lag in range(1, lags):
            ahead = moved_rows(d_pre, -lag, seq)
            d_vals = d_vals + taps_ref[lag : lag + 1, part] * ahead
            set_grads(lag, part, jnp.sum(ahead * values, axis=0, keepdims=True))
        rounded = d_vals.astype(BF16)
        vals_ref[:, part] = rounded
        product = rounded.astype(F32) * inner_ref[:, part]
        for lane in range(0, block, LANES):
            sums = sums + product[:, lane : lane + LANES]
    return jnp.broadcast_to(jnp.sum(sums, axis=1, keepdims=True), (rows, LANES))


def first_kernel(
    seq,
    me_slot,
    sections,
    idx_ref,
    keep_ref,
    dy_ref,
    layer_ref,
    conv_ref,
    gain_ref,
    taps_ref,
    wo_hbm,
    wi_hbm,
    *refs,
):
    vals_ref, grads_ref, sums_ref, inner_ref, slope_ref, rows_ref, *refs = refs
    normed_ref, inv_ref, up_ref, gain_part_ref, *refs = refs
    flag_refs, refs = refs[:sections], refs[sections:]
    *weights, top_ref, acc_ref, sem = refs
    blocks = len(weights) // 2
    for step, flag_ref in enumerate(flag_refs):
        flag = jnp.where(idx_ref[me_slot + blocks + step] == 1, 1.0, 0.0)
        flag_ref[...] = jnp.full(flag_ref.shape, flag, F32)
    wo_refs, wi_refs = weights[:blocks], weights[blocks:]
    full = idx_ref[0]
    model = gain_ref.shape[1]
    width = up_ref.shape[1]
    channels = taps_ref.shape[1]
    lags = taps_ref.shape[0]
    short = acc_ref.shape[0] - seq
    copies = []
    for i in range(blocks):
        columns = pl.ds(pl.multiple_of(idx_ref[me_slot + i] * width, width), width)
        copies.append(pltpu.make_async_copy(wo_hbm.at[:, columns], wo_refs[i], sem.at[i]))
    for i in range(blocks):
        features = pl.ds(pl.multiple_of(idx_ref[me_slot + i] * width, width), width)
        copies.append(pltpu.make_async_copy(wi_hbm.at[features, :], wi_refs[i], sem.at[blocks + i]))
    for copy in copies:
        copy.start()

    def live(ref, part):
        head = ref[full, :, part].astype(F32)
        tail = ref[1 - full, :short, part].astype(F32)
        return jnp.concatenate([head, tail], axis=0)

    keep = keep_ref[:, 0:1]
    squares = jnp.zeros((seq + short, LANES), F32)
    chunk = min(1024, width)
    for i in range(model // chunk):
        part = slice(i * chunk, (i + 1) * chunk)
        top_ref[:, part] = (live(dy_ref, part) * keep).astype(BF16)
        values = live(layer_ref, part)
        values = values * values
        for lane in range(0, chunk, LANES):
            squares = squares + values[:, lane : lane + LANES]
    mean = jnp.sum(squares, axis=1, keepdims=True) * (1.0 / model)
    inv = lax.rsqrt(mean + EPSILON)
    inv_ref[...] = jnp.broadcast_to(inv, inv_ref.shape)
    mine = pl.ds(pl.multiple_of(idx_ref[me_slot] * width, width), width)
    normed_ref[...] = live(layer_ref, mine) * inv
    up_ref[...] = top_ref[:, mine]
    gain_part_ref[...] = gain_ref[:, mine]
    block = 256 if channels % 256 == 0 else LANES
    for at in range(0, channels, block):
        part = slice(at, at + block)
        values = live(conv_ref, part)
        rows_ref[:, part] = values
        pre_act = taps_ref[0:1, part] * values
        for lag in range(1, lags):
            pre_act = pre_act + taps_ref[lag : lag + 1, part] * moved_rows(values, lag, seq)
        gate = 1.0 / (1.0 + jnp.exp(-pre_act))
        slope_ref[:, part] = gate * (1.0 + pre_act * (1.0 - gate))

    half = min(512, width)
    for i in range(blocks):
        copies[i].wait()
        for at in range(0, width, half):
            part = pl.ds(pl.multiple_of(idx_ref[me_slot + i] * width + at, half), half)
            term = lax.dot_general(
                top_ref[:, part], wo_refs[i][:, at : at + half], NT, preferred_element_type=F32
            )
            if i + at == 0:
                acc_ref[...] = term
            else:
                acc_ref[...] += term
    for i in range(blocks):
        copies[blocks + i].wait()
        for at in range(0, width, half):
            part = pl.ds(pl.multiple_of(idx_ref[me_slot + i] * width + at, half), half)
            scaled = (live(layer_ref, part) * inv * gain_ref[:, part]).astype(BF16)
            term = lax.dot_general(
                scaled, wi_refs[i][at : at + half, :], NN, preferred_element_type=F32
            )
            if i + at == 0:
                inner_ref[...] = term
            else:
                inner_ref[...] += term
    sums_ref[...] = conv_backward(
        seq, acc_ref, slope_ref, rows_ref, taps_ref, inner_ref, vals_ref, grads_ref
    )


def act_kernel(seq, count, first, last, *refs):
    pieces, wo_refs, refs = refs[:count], refs[count : 2 * count], refs[2 * count :]
    if not first:
        so_far, refs = refs[0], refs[1:]
    if last:
        slope_ref, rows_ref, taps_ref, inner_ref, kept_ref, working_ref, *refs = refs
        vals_ref, grads_ref, sums_ref, acc_ref = refs
    else:
        (acc_ref,) = refs
    channels = acc_ref.shape[1]
    block = 256 if channels % 256 == 0 else LANES
    for at in range(0, channels, block):
        part = slice(at, at + block)
        total = None if first else so_far[:, part]
        for piece, wo_ref in zip(pieces, wo_refs):
            term = lax.dot_general(piece[...], wo_ref[part, :], NT, preferred_element_type=F32)
            total = term if total is None else total + term
        acc_ref[:, part] = total
    if last:
        active = working_ref[0:1, 0:1] > 0.0
        sums_ref[...] = conv_backward(
            seq, acc_ref, slope_ref, rows_ref, taps_ref, inner_ref, vals_ref, grads_ref, active, kept_ref
        )


def block_product(vals_ref, wi_ref, at, chunk):
    return lax.dot_general(
        vals_ref[...], wi_ref[at : at + chunk, :], NT, preferred_element_type=F32
    )


def split_sums(sums):
    high = sums.astype(BF16)
    low = (sums - high.astype(F32)).astype(BF16)
    lane = lax.broadcasted_iota(jnp.int32, sums.shape, 1)
    return jnp.where(lane < LANES // 2, high.astype(F32), low.astype(F32)).astype(BF16)


def joined_sums(block, width):
    high = block[:, width : width + 1].astype(F32)
    return high + block[:, width + LANES // 2 : width + LANES // 2 + 1].astype(F32)


def other_blocks_kernel(vals_ref, sums_ref, *refs):
    wi_refs, out_ref = refs[:-1], refs[-1]
    width = out_ref.shape[2] - LANES
    chunk = min(512, width)
    for number, wi_ref in enumerate(wi_refs):
        for at in range(0, width, chunk):
            term = block_product(vals_ref, wi_ref, at, chunk)
            out_ref[number, :, at : at + chunk] = term.astype(BF16)
        out_ref[number, :, width:] = split_sums(sums_ref[...])


def own_blocks_kernel(chips, picks, vals_ref, sums_ref, *refs):
    count = len(chips)
    wi_refs, recv_refs, out_refs = refs[:count], refs[count:-count], refs[-count:]
    width = out_refs[0].shape[1] - LANES
    chunk = min(512, width)
    for chip, pick, wi_ref, out_ref in zip(chips, picks, wi_refs, out_refs):
        for at in range(0, width, chunk):
            term = block_product(vals_ref, wi_ref, at, chunk)
            for number, slot in pick:
                part = slice(at, at + chunk)
                recv = recv_refs[number]
                recv = recv[:, part] if slot is None else recv[slot, :, part]
                term = term + recv.astype(F32)
            out_ref[:, at : at + chunk] = term.astype(out_ref.dtype)
        sums = sums_ref[...]
        for number, slot in pick:
            recv = recv_refs[number]
            sums = sums + joined_sums(recv if slot is None else recv.at[slot], width)
        out_ref[:, width:] = split_sums(sums) if chip else sums


def norm_kernel(
    model,
    first,
    last,
    own_ref,
    a_ref,
    b_ref,
    normed_ref,
    inv_ref,
    gain_ref,
    up_ref,
    *refs,
):
    if not first:
        earlier_ref, gains_ref, working_ref, *refs = refs
        active = working_ref[0:1, 0:1] > 0.0
    if last:
        (out_ref,) = refs
    else:
        out_ref, kept_ref, sum_ref = refs
    rows, width = normed_ref.shape
    sums = own_ref[:, width : width + 1]
    for ref in (a_ref, b_ref):
        sums = sums + joined_sums(ref, width)
    mean = sums * (1.0 / model)
    inv = inv_ref[:, 0:1]
    chunk = min(512, width)
    for at in range(0, width, chunk):
        part = slice(at, at + chunk)
        d_norm = own_ref[:, part]
        for ref in (a_ref, b_ref):
            d_norm = d_norm + ref[:, part].astype(F32)
        normed = normed_ref[:, part]
        d_in = inv * (d_norm * gain_ref[:, part] - normed * mean)
        grad = up_ref[:, part].astype(F32) + d_in
        gains = jnp.sum(d_norm * normed, axis=0, keepdims=True)
        kept = grad
        if not first:
            kept = jnp.where(active, grad, earlier_ref[:, part].astype(F32))
            gains = jnp.where(active, gains, gains_ref[:, part])
        if last:
            high = gains.astype(BF16).astype(F32)
            row = lax.broadcasted_iota(jnp.int32, (GAIN_ROWS, chunk), 0)
            both = jnp.where(row == 0, high, jnp.where(row == 1, gains - high, 0.0))
            out_ref[:rows, part] = kept.astype(BF16)
            out_ref[rows:, part] = both.astype(BF16)
        else:
            out_ref[:, part] = grad.astype(BF16)
            kept_ref[:, part] = kept.astype(BF16)
            sum_ref[:, part] = gains


def assemble_kernel(seq, rows, me_slot, idx_ref, *refs):
    pieces, (out_ref, gain_ref) = refs[:-2], refs[-2:]
    width = pieces[0].shape[1]
    full = idx_ref[0]
    short = rows - seq
    for number, piece in enumerate(pieces):
        columns = pl.ds(pl.multiple_of(idx_ref[me_slot + number] * width, width), width)
        out_ref[full, :, columns] = piece[:seq]
        out_ref[1 - full, :short, columns] = piece[seq:rows]
        out_ref[1 - full, short:, columns] = jnp.zeros((seq - short, width), BF16)
        gains = piece[rows:].astype(F32)
        gain_ref[:, columns] = gains[0:1] + gains[1:2]


def local(dy_top, loss_mask, counts, layer_in, conv_in, norm_gain, conv_weight, in_proj, out_proj):
    sections = lax.axis_size("section")
    tensors = lax.axis_size("tensor")
    section = lax.axis_index("section").astype(jnp.int32)
    me = lax.axis_index("tensor").astype(jnp.int32)
    seq, model = dy_top.shape[1:]
    short = seq // 2
    rows = seq + short
    parts = tensors // CHIPS
    width = model // tensors
    w_in, w_out, taps = in_proj[0], out_proj[0], conv_weight[0]
    lags, channels = taps.shape

    full = jnp.where(counts[0] == seq, 0, 1).astype(jnp.int32)
    positions = jnp.arange(seq, dtype=jnp.int32)
    keep = ((loss_mask == 1) & (positions[None, :] < counts[:, None])).astype(F32)
    keep_full = jnp.where(full == 0, keep[0], keep[1])
    keep_short = jnp.where(full == 0, keep[1], keep[0])[:short]
    keep_rows = jnp.broadcast_to(
        jnp.concatenate([keep_full, keep_short])[:, None], (rows, LANES)
    )

    me_slot = 1

    blocks = jnp.arange(tensors, dtype=jnp.int32) ^ me
    working = (jnp.arange(sections) == sections - 1 - section).astype(jnp.int32)
    table = jnp.concatenate([full[None], blocks, working])

    def across(x, chip):
        return lax.ppermute(x, "tensor", [(i, i ^ (chip * parts)) for i in range(tensors)])

    def sideways(x, side):
        return lax.ppermute(x, "tensor", [(i, i ^ side) for i in range(tensors)])

    def below(x):
        return lax.ppermute(x, "section", [(i, i - 1) for i in range(1, sections)])

    sides = range(1, parts)
    order = (3, 1, 2)

    def product_cost(count, as_rows=512):
        return dict(
            flops=2 * as_rows * channels * width * count,
            moved=2 * channels * width * count,
        )

    vals_shape = SDS((rows, channels), BF16)
    grads_shape = SDS((lags, channels), F32)
    sums_shape = SDS((rows, LANES), F32)
    channel_shape = SDS((rows, channels), F32)
    block_rows = [(channels, width)] * tensors + [(width, channels)] * tensors
    d_vals, tap_grads, sums, inner, slope, conv_rows, normed, inv, upstream, gain, *rest = kernel_call(
        functools.partial(first_kernel, seq, me_slot, sections),
        (
            vals_shape,
            grads_shape,
            sums_shape,
            channel_shape,
            channel_shape,
            channel_shape,
            SDS((rows, width), F32),
            SDS((rows, LANES), F32),
            SDS((rows, width), BF16),
            SDS((1, width), F32),
        )
        + (SDS((8, LANES), F32),) * sections
        + tuple(pltpu.VMEM(shape, BF16) for shape in block_rows),
        [table, keep_rows, dy_top, layer_in[0], conv_in[0], norm_gain, taps, w_out, w_in],
        [
            pltpu.VMEM((rows, model), BF16),
            pltpu.VMEM((rows, channels), F32),
            pltpu.SemaphoreType.DMA((2 * tensors,)),
        ],
        limit=12,
        flops=4 * rows * channels * model,
        moved=4 * channels * model,
        specs=[SMEM] + [VMEM] * 6 + [HBM] * 2,
    )
    flags, weights = rest[:sections], rest[sections:]
    wo, wi = weights[:tensors], weights[tensors:]

    def activation(step, own, taps_kept):
        far = {chip: across(own, chip) for chip in order}
        far[0] = own
        plan = (0,) + order
        total, waiting = None, []
        for number in range(len(plan) + 1):
            first, last = number == 0, number == len(plan)
            group, waiting = waiting, []
            if not last:
                chip = plan[number]
                piece = far[chip]
                if not first:
                    piece, total = lax.optimization_barrier((piece, total))
                group.append((piece, chip, 0))
                waiting = [(sideways(piece, side), chip, side) for side in sides]
            operands = [piece for piece, _, _ in group]
            operands += [resident(wo[chip * parts + side]) for _, chip, side in group]
            operands += [] if first else [total]
            operands += [slope, conv_rows, taps, inner, taps_kept, flags[step]] if last else []
            total = kernel_call(
                functools.partial(act_kernel, seq, len(group), first, last),
                (vals_shape, grads_shape, sums_shape) if last else channel_shape,
                operands,
                [pltpu.VMEM((rows, channels), F32)] if last else [],
                **product_cost(len(group), 512),
            )
        return total

    def summed(vals, row_sums):
        def for_others(chips):
            return [
                sideways(
                    kernel_call(
                        other_blocks_kernel,
                        SDS((len(chips), rows, width + LANES), BF16),
                        [vals, row_sums] + [resident(wi[chip * parts + side]) for chip in chips],
                        **product_cost(len(chips), 64),
                    ),
                    side,
                )
                for side in sides
            ]

        def for_own(chips, batches, after=None, arrays=()):
            arrays = list(arrays)
            picks = [[(number, None) for number in range(len(arrays))] for _ in chips]
            for batch_chips, batch in batches:
                for array in batch:
                    for slot, chip in enumerate(batch_chips):
                        if chip in chips:
                            picks[chips.index(chip)].append((len(arrays), slot))
                    arrays.append(array)
            return kernel_call(
                functools.partial(own_blocks_kernel, chips, picks),
                tuple(SDS((rows, width + LANES), BF16 if chip else F32) for chip in chips),
                [vals, row_sums] + [resident(wi[chip * parts]) for chip in chips] + arrays,
                after=after,
                **product_cost(len(chips), 64),
            )

        early, late = (order[0], order[1]), (order[2], 0)
        sent_early = (early, for_others(early))
        sent_late = (late, for_others(late))
        (third,) = for_own(order[:1], [sent_early])
        first, second = for_own(order[1:], [sent_early, sent_late], third)
        arrived = across(third, order[0])
        far = [across(first, order[1]), across(second, order[2])]
        return for_own((0,), [sent_late], first, [arrived]) + tuple(far)

    taps_kept = tap_grads
    for step in range(sections):
        first, last = step == 0, step == sections - 1
        if not first:
            d_vals, taps_kept, sums = activation(step, upstream, taps_kept)
        terms = summed(d_vals, sums)
        block = SDS((rows, width), BF16)
        results = kernel_call(
            functools.partial(norm_kernel, model, first, last),
            SDS((rows + GAIN_ROWS, width), BF16) if last else (block, block, SDS((1, width), F32)),
            list(terms) + [normed, inv, gain, upstream] + ([] if first else [kept, gains, flags[step]]),
        )
        if last:
            own = results
        else:
            grad, kept, gains = results
            upstream = below(grad)

    far = [own] + [across(own, chip) for chip in range(1, CHIPS)]
    pieces = []
    for piece in far:
        pieces += [piece] + [sideways(piece, side) for side in sides]
    result, gain_grads = kernel_call(
        functools.partial(assemble_kernel, seq, rows, me_slot),
        (SDS((2, seq, model), BF16), SDS((1, model), F32)),
        [table] + pieces,
        limit=8,
    )
    return (result[None], gain_grads, taps_kept[None])


def solution(mesh):
    placed = (
        P(),
        P(),
        P(),
        P("section", None, None, None),
        P("section", None, None, "tensor"),
        P("section", None),
        P("section", None, "tensor"),
        P("section", None, "tensor"),
        P("section", "tensor", None),
    )
    return jax.shard_map(
        local,
        mesh=mesh,
        in_specs=placed,
        out_specs=(
            P("section", None, None, None),
            P("section", None),
            P("section", None, "tensor"),
        ),
        check_vma=False,
    )
```

```python
import functools

import jax
import jax.numpy as jnp
from jax import lax
from jax.experimental import pallas as pl
from jax.experimental.pallas import tpu as pltpu
from jax.sharding import PartitionSpec as P

EPSILON = 1e-05
CHIPS = 4
LANES = 128
GAIN_ROWS = 8
F32 = jnp.float32
BF16 = jnp.bfloat16
NT = (((1,), (1,)), ((), ()))
NN = (((1,), (0,)), ((), ()))
VMEM = pl.BlockSpec(memory_space=pltpu.VMEM)
SMEM = pl.BlockSpec(memory_space=pltpu.SMEM)
HBM = pl.BlockSpec(memory_space=pltpu.HBM)
ANY = pl.BlockSpec(memory_space=pl.ANY)
MIB = 1 << 20
SDS = jax.ShapeDtypeStruct


def kernel_call(
    body, out_shape, operands, scratch=(), limit=4, flops=0, moved=0, specs=None, after=None, out_specs=None, aliases=None
):
    specs = specs or [SMEM if op.dtype == jnp.int32 else VMEM for op in operands]
    if after is not None:
        operands, specs = [after] + operands, [ANY] + specs
        body = functools.partial(skip_first, body)
    return pl.pallas_call(
        body,
        in_specs=specs,
        out_specs=out_specs
        or jax.tree.map(lambda _: VMEM, out_shape, is_leaf=lambda s: hasattr(s, "shape")),
        out_shape=out_shape,
        scratch_shapes=list(scratch),
        input_output_aliases=aliases or {},
        compiler_params=pltpu.CompilerParams(vmem_limit_bytes=limit * MIB),
        cost_estimate=pl.CostEstimate(flops=flops, bytes_accessed=moved, transcendentals=0),
    )(*operands)


def skip_first(body, _, *refs):
    body(*refs)


def resident(weights):
    return pltpu.with_memory_space_constraint(weights, pltpu.VMEM)


def moved_rows(values, by, seq):
    rows = values.shape[0]
    row = lax.broadcasted_iota(jnp.int32, values.shape, 0)
    if by > 0:
        keep = (row >= by) & ((row < seq) | (row >= seq + by))
        turned = pltpu.roll(values, by, 0)
    else:
        keep = (row < rows + by) & ((row < seq + by) | (row >= seq))
        turned = pltpu.roll(values, rows + by, 0)
    return jnp.where(keep, turned, 0.0)


def conv_backward(
    seq, acc_ref, slope_ref, rows_ref, taps_ref, inner_ref, vals_ref, grads_ref, active=None, kept_ref=None
):
    rows, channels = acc_ref.shape
    lags = taps_ref.shape[0]
    block = 256 if channels % 256 == 0 else LANES
    sums = jnp.zeros((rows, LANES), F32)

    def set_grads(lag, part, value):
        row = slice(lag, lag + 1)
        if kept_ref is not None:
            value = jnp.where(active, value, kept_ref[row, part])
        grads_ref[row, part] = value

    for at in range(0, channels, block):
        part = slice(at, at + block)
        d_pre = acc_ref[:, part] * slope_ref[:, part]
        values = rows_ref[:, part]
        d_vals = taps_ref[0:1, part] * d_pre
        set_grads(0, part, jnp.sum(d_pre * values, axis=0, keepdims=True))
        for lag in range(1, lags):
            ahead = moved_rows(d_pre, -lag, seq)
            d_vals = d_vals + taps_ref[lag : lag + 1, part] * ahead
            set_grads(lag, part, jnp.sum(ahead * values, axis=0, keepdims=True))
        rounded = d_vals.astype(BF16)
        vals_ref[:, part] = rounded
        product = rounded.astype(F32) * inner_ref[:, part]
        for lane in range(0, block, LANES):
            sums = sums + product[:, lane : lane + LANES]
    return jnp.broadcast_to(jnp.sum(sums, axis=1, keepdims=True), (rows, LANES))


def first_kernel(
    seq,
    me_slot,
    sections,
    idx_ref,
    counts_ref,
    *refs,
):
    sources, refs = refs[:6], refs[6:]
    wo_hbm, wi_hbm, *refs = refs
    vals_ref, grads_ref, sums_ref, inner_ref, slope_ref, rows_ref, *refs = refs
    normed_ref, inv_ref, up_ref, gain_part_ref, *refs = refs
    full_ref, *refs = refs
    flag_refs, refs = refs[:sections], refs[sections:]
    weights, refs = refs[:-10], refs[-10:]
    dy_ref, mask_ref, layer_ref, conv_ref, gain_ref, taps_ref, *refs = refs
    top_ref, scaled_ref, acc_ref, sem = refs
    blocks = len(weights) // 2
    wo_refs, wi_refs = weights[:blocks], weights[blocks:]
    model = gain_ref.shape[1]
    width = up_ref.shape[1]
    lags, channels = taps_ref.shape
    rows = acc_ref.shape[0]
    short = rows - seq

    def columns(i):
        return pl.ds(pl.multiple_of(idx_ref[me_slot + i] * width, width), width)

    held = [mask_ref, dy_ref, layer_ref, conv_ref, gain_ref, taps_ref]
    small = [
        pltpu.make_async_copy(source, ref, sem.at[2 * blocks + i])
        for i, (source, ref) in enumerate(zip(sources, held))
    ]
    out_copies = [
        pltpu.make_async_copy(wo_hbm.at[:, columns(i)], wo_refs[i], sem.at[i])
        for i in range(blocks)
    ]
    in_copies = [
        pltpu.make_async_copy(wi_hbm.at[columns(i), :], wi_refs[i], sem.at[blocks + i])
        for i in range(blocks)
    ]
    order = small[:2] + out_copies[:1] + small[2:]
    for i in range(blocks):
        order += in_copies[i : i + 1] + out_copies[i + 1 : i + 2]
    for copy in order:
        copy.start()

    for step, flag_ref in enumerate(flag_refs):
        flag = jnp.where(idx_ref[me_slot + blocks + step] == 1, 1.0, 0.0)
        flag_ref[...] = jnp.full(flag_ref.shape, flag, F32)
    full = jnp.where(counts_ref[0] == seq, 0, 1)
    full_ref[...] = jnp.full(full_ref.shape, jnp.where(full == 1, 1.0, 0.0), F32)

    def live(ref, part):
        head = ref[full, :, part].astype(F32)
        tail = ref[1 - full, :short, part].astype(F32)
        return jnp.concatenate([head, tail], axis=0)

    def keep_column(batch):
        lane = lax.broadcasted_iota(jnp.int32, (seq, seq), 1)
        row = lax.broadcasted_iota(jnp.int32, (seq, seq), 0)
        mask = jnp.broadcast_to(mask_ref[pl.ds(batch, 1), :], (seq, seq))
        on = (mask == 1) & (lane < counts_ref[batch]) & (lane == row)
        return jnp.sum(jnp.where(on, 1.0, 0.0), axis=1, keepdims=True)

    small[0].wait()
    keep = jnp.concatenate([keep_column(full), keep_column(1 - full)[:short]], axis=0)

    def make_top(i):
        top_ref[i] = (live(dy_ref, columns(i)) * keep).astype(BF16)

    block = 256 if channels % 256 == 0 else LANES
    slope_parts = list(range(0, channels, block))

    def make_slope(at):
        part = slice(at, at + block)
        values = live(conv_ref, part)
        rows_ref[:, part] = values
        pre_act = taps_ref[0:1, part] * values
        for lag in range(1, lags):
            pre_act = pre_act + taps_ref[lag : lag + 1, part] * moved_rows(values, lag, seq)
        gate = 1.0 / (1.0 + jnp.exp(-pre_act))
        slope_ref[:, part] = gate * (1.0 + pre_act * (1.0 - gate))

    def make_scaled(i):
        scaled_ref[i % 2] = (live(layer_ref, columns(i)) * gain_ref[:, columns(i)]).astype(BF16)

    small[1].wait()
    make_top(0)
    up_ref[...] = top_ref[0]
    squares = jnp.zeros((rows, LANES), F32)
    for i in range(blocks):
        out_copies[i].wait()
        for at in range(0, channels, block):
            part = slice(at, at + block)
            term = lax.dot_general(top_ref[i], wo_refs[i][part, :], NT, preferred_element_type=F32)
            acc_ref[:, part] = term if i == 0 else acc_ref[:, part] + term
        if i == 0:
            for copy in small[2:]:
                copy.wait()
            make_scaled(0)
        if i + 1 < blocks:
            make_top(i + 1)
        values = live(layer_ref, slice(i * width, (i + 1) * width))
        values = values * values
        for lane in range(0, width, LANES):
            squares = squares + values[:, lane : lane + LANES]
        in_copies[i].wait()
        for at in range(0, channels, block):
            part = slice(at, at + block)
            term = lax.dot_general(
                scaled_ref[i % 2], wi_refs[i][:, part], NN, preferred_element_type=F32
            )
            inner_ref[:, part] = term if i == 0 else inner_ref[:, part] + term
        if i + 1 < blocks:
            make_scaled(i + 1)
        for at in slope_parts[i::blocks]:
            make_slope(at)
    mean = jnp.sum(squares, axis=1, keepdims=True) * (1.0 / model)
    inv = lax.rsqrt(mean + EPSILON)
    inv_ref[...] = jnp.broadcast_to(inv, inv_ref.shape)
    normed_ref[...] = live(layer_ref, columns(0)) * inv
    gain_part_ref[...] = gain_ref[:, columns(0)]
    for at in range(0, channels, block):
        part = slice(at, at + block)
        inner_ref[:, part] = inner_ref[:, part] * inv
    sums_ref[...] = conv_backward(
        seq, acc_ref, slope_ref, rows_ref, taps_ref, inner_ref, vals_ref, grads_ref
    )


def act_kernel(seq, count, first, last, *refs):
    pieces, wo_refs, refs = refs[:count], refs[count : 2 * count], refs[2 * count :]
    if not first:
        so_far, refs = refs[0], refs[1:]
    if last:
        slope_ref, rows_ref, taps_ref, inner_ref, kept_ref, working_ref, *refs = refs
        vals_ref, grads_ref, sums_ref, acc_ref = refs
    else:
        (acc_ref,) = refs
    channels = acc_ref.shape[1]
    block = 256 if channels % 256 == 0 else LANES
    for at in range(0, channels, block):
        part = slice(at, at + block)
        total = None if first else so_far[:, part]
        for piece, wo_ref in zip(pieces, wo_refs):
            term = lax.dot_general(piece[...], wo_ref[part, :], NT, preferred_element_type=F32)
            total = term if total is None else total + term
        acc_ref[:, part] = total
    if last:
        active = working_ref[0:1, 0:1] > 0.0
        sums_ref[...] = conv_backward(
            seq, acc_ref, slope_ref, rows_ref, taps_ref, inner_ref, vals_ref, grads_ref, active, kept_ref
        )


def block_product(vals_ref, wi_ref, at, chunk):
    return lax.dot_general(
        vals_ref[...], wi_ref[at : at + chunk, :], NT, preferred_element_type=F32
    )


def split_sums(sums):
    high = sums.astype(BF16)
    low = (sums - high.astype(F32)).astype(BF16)
    lane = lax.broadcasted_iota(jnp.int32, sums.shape, 1)
    return jnp.where(lane < LANES // 2, high.astype(F32), low.astype(F32)).astype(BF16)


def joined_sums(block, width):
    high = block[:, width : width + 1].astype(F32)
    return high + block[:, width + LANES // 2 : width + LANES // 2 + 1].astype(F32)


def other_blocks_kernel(vals_ref, sums_ref, *refs):
    wi_refs, out_ref = refs[:-1], refs[-1]
    width = out_ref.shape[2] - LANES
    chunk = min(512, width)
    for number, wi_ref in enumerate(wi_refs):
        for at in range(0, width, chunk):
            term = block_product(vals_ref, wi_ref, at, chunk)
            out_ref[number, :, at : at + chunk] = term.astype(BF16)
        out_ref[number, :, width:] = split_sums(sums_ref[...])


def own_blocks_kernel(chips, picks, vals_ref, sums_ref, *refs):
    count = len(chips)
    wi_refs, recv_refs, out_refs = refs[:count], refs[count:-count], refs[-count:]
    width = out_refs[0].shape[1] - LANES
    chunk = min(512, width)
    for chip, pick, wi_ref, out_ref in zip(chips, picks, wi_refs, out_refs):
        for at in range(0, width, chunk):
            term = block_product(vals_ref, wi_ref, at, chunk)
            for number, slot in pick:
                part = slice(at, at + chunk)
                recv = recv_refs[number]
                recv = recv[:, part] if slot is None else recv[slot, :, part]
                term = term + recv.astype(F32)
            out_ref[:, at : at + chunk] = term.astype(out_ref.dtype)
        sums = sums_ref[...]
        for number, slot in pick:
            recv = recv_refs[number]
            sums = sums + joined_sums(recv if slot is None else recv.at[slot], width)
        out_ref[:, width:] = split_sums(sums) if chip else sums


def norm_kernel(
    model,
    first,
    last,
    own_ref,
    a_ref,
    b_ref,
    normed_ref,
    inv_ref,
    gain_ref,
    up_ref,
    *refs,
):
    if not first:
        earlier_ref, gains_ref, working_ref, *refs = refs
        active = working_ref[0:1, 0:1] > 0.0
    if last:
        (out_ref,) = refs
    else:
        out_ref, kept_ref, sum_ref = refs
    rows, width = normed_ref.shape
    sums = own_ref[:, width : width + 1]
    for ref in (a_ref, b_ref):
        sums = sums + joined_sums(ref, width)
    mean = sums * (1.0 / model)
    inv = inv_ref[:, 0:1]
    chunk = min(512, width)
    for at in range(0, width, chunk):
        part = slice(at, at + chunk)
        d_norm = own_ref[:, part]
        for ref in (a_ref, b_ref):
            d_norm = d_norm + ref[:, part].astype(F32)
        normed = normed_ref[:, part]
        d_in = inv * (d_norm * gain_ref[:, part] - normed * mean)
        grad = up_ref[:, part].astype(F32) + d_in
        gains = jnp.sum(d_norm * normed, axis=0, keepdims=True)
        kept = grad
        if not first:
            kept = jnp.where(active, grad, earlier_ref[:, part].astype(F32))
            gains = jnp.where(active, gains, gains_ref[:, part])
        if last:
            high = gains.astype(BF16).astype(F32)
            row = lax.broadcasted_iota(jnp.int32, (GAIN_ROWS, chunk), 0)
            both = jnp.where(row == 0, high, jnp.where(row == 1, gains - high, 0.0))
            out_ref[:rows, part] = kept.astype(BF16)
            out_ref[rows:, part] = both.astype(BF16)
        else:
            out_ref[:, part] = grad.astype(BF16)
            kept_ref[:, part] = kept.astype(BF16)
            sum_ref[:, part] = gains


def assemble_kernel(seq, rows, distances, first, full_ref, *refs):
    if not first:
        refs = refs[2:]
    pieces, (out_ref, gain_ref, zero_ref, sem) = refs[:-4], refs[-4:]
    me = lax.axis_index("tensor")
    width = pieces[0].shape[1]
    full = jnp.where(jnp.max(full_ref[...]) > 0.5, 1, 0)
    short = rows - seq
    copies = []
    if first:
        zero_ref[...] = jnp.zeros(zero_ref.shape, BF16)
        copies.append(pltpu.make_async_copy(zero_ref, out_ref.at[1 - full, short:], sem.at[0]))
    for distance, piece in zip(distances, pieces):
        columns = pl.ds(pl.multiple_of((me ^ distance) * width, width), width)
        ends = (
            (piece.at[:seq], out_ref.at[full, :, columns]),
            (piece.at[seq:rows], out_ref.at[1 - full, :short, columns]),
        )
        for source, target in ends:
            copies.append(pltpu.make_async_copy(source, target, sem.at[len(copies)]))
    for copy in copies:
        copy.start()
    for distance, piece in zip(distances, pieces):
        gains = piece[rows:].astype(F32)
        gain_ref[pl.ds(me ^ distance, 1), :] = gains[0:1] + gains[1:2]
    for copy in copies:
        copy.wait()


def local(dy_top, loss_mask, counts, layer_in, conv_in, norm_gain, conv_weight, in_proj, out_proj):
    sections = lax.axis_size("section")
    tensors = lax.axis_size("tensor")
    section = lax.axis_index("section").astype(jnp.int32)
    me = lax.axis_index("tensor").astype(jnp.int32)
    seq, model = dy_top.shape[1:]
    short = seq // 2
    rows = seq + short
    parts = tensors // CHIPS
    width = model // tensors
    w_in, w_out, taps = in_proj[0], out_proj[0], conv_weight[0]
    lags, channels = taps.shape

    me_slot = 0

    blocks = jnp.arange(tensors, dtype=jnp.int32) ^ me
    working = (jnp.arange(sections) == sections - 1 - section).astype(jnp.int32)
    table = jnp.concatenate([blocks, working])

    def across(x, chip):
        return lax.ppermute(x, "tensor", [(i, i ^ (chip * parts)) for i in range(tensors)])

    def sideways(x, side):
        return lax.ppermute(x, "tensor", [(i, i ^ side) for i in range(tensors)])

    def below(x):
        return lax.ppermute(x, "section", [(i, i - 1) for i in range(1, sections)])

    sides = range(1, parts)
    order = (3, 1, 2)

    def product_cost(count, as_rows=512):
        return dict(
            flops=2 * as_rows * channels * width * count,
            moved=2 * channels * width * count,
        )

    vals_shape = SDS((rows, channels), BF16)
    grads_shape = SDS((lags, channels), F32)
    sums_shape = SDS((rows, LANES), F32)
    channel_shape = SDS((rows, channels), F32)
    block_rows = [(channels, width)] * tensors + [(width, channels)] * tensors
    d_vals, tap_grads, sums, inner, slope, conv_rows, normed, inv, upstream, gain, *rest = kernel_call(
        functools.partial(first_kernel, seq, me_slot, sections),
        (
            vals_shape,
            grads_shape,
            sums_shape,
            channel_shape,
            channel_shape,
            channel_shape,
            SDS((rows, width), F32),
            SDS((rows, LANES), F32),
            SDS((rows, width), BF16),
            SDS((1, width), F32),
        )
        + (SDS((8, LANES), F32),) * (1 + sections)
        + tuple(pltpu.VMEM(shape, BF16) for shape in block_rows),
        [table, counts]
        + [
            pltpu.with_memory_space_constraint(source, pltpu.HBM)
            for source in (
                loss_mask, dy_top, layer_in[0], conv_in[0], norm_gain, taps, w_out, w_in
            )
        ],
        [
            pltpu.VMEM(dy_top.shape, BF16),
            pltpu.VMEM(loss_mask.shape, jnp.int32),
            pltpu.VMEM(layer_in.shape[1:], BF16),
            pltpu.VMEM(conv_in.shape[1:], BF16),
            pltpu.VMEM(norm_gain.shape, F32),
            pltpu.VMEM(taps.shape, F32),
            pltpu.VMEM((tensors, rows, width), BF16),
            pltpu.VMEM((2, rows, width), BF16),
            pltpu.VMEM((rows, channels), F32),
            pltpu.SemaphoreType.DMA((2 * tensors + 6,)),
        ],
        limit=12,
        flops=4 * rows * channels * model,
        moved=4 * channels * model,
        specs=[SMEM, SMEM] + [HBM] * 8,
    )
    full, *rest = rest
    flags, weights = rest[:sections], rest[sections:]
    wo, wi = weights[:tensors], weights[tensors:]

    def activation(step, own, taps_kept):
        far = {chip: across(own, chip) for chip in order}
        far[0] = own
        plan = (0,) + order
        total, waiting = None, []
        for number in range(len(plan) + 1):
            first, last = number == 0, number == len(plan)
            group, waiting = waiting, []
            if not last:
                chip = plan[number]
                piece = far[chip]
                if not first:
                    piece, total = lax.optimization_barrier((piece, total))
                group.append((piece, chip, 0))
                waiting = [(sideways(piece, side), chip, side) for side in sides]
            operands = [piece for piece, _, _ in group]
            operands += [resident(wo[chip * parts + side]) for _, chip, side in group]
            operands += [] if first else [total]
            operands += [slope, conv_rows, taps, inner, taps_kept, flags[step]] if last else []
            total = kernel_call(
                functools.partial(act_kernel, seq, len(group), first, last),
                (vals_shape, grads_shape, sums_shape) if last else channel_shape,
                operands,
                [pltpu.VMEM((rows, channels), F32)] if last else [],
                **product_cost(len(group), 512),
            )
        return total

    def summed(vals, row_sums):
        def for_others(chips):
            return [
                sideways(
                    kernel_call(
                        other_blocks_kernel,
                        SDS((len(chips), rows, width + LANES), BF16),
                        [vals, row_sums] + [resident(wi[chip * parts + side]) for chip in chips],
                        **product_cost(len(chips), 64),
                    ),
                    side,
                )
                for side in sides
            ]

        def for_own(chips, batches, after=None, arrays=()):
            arrays = list(arrays)
            picks = [[(number, None) for number in range(len(arrays))] for _ in chips]
            for batch_chips, batch in batches:
                for array in batch:
                    for slot, chip in enumerate(batch_chips):
                        if chip in chips:
                            picks[chips.index(chip)].append((len(arrays), slot))
                    arrays.append(array)
            return kernel_call(
                functools.partial(own_blocks_kernel, chips, picks),
                tuple(SDS((rows, width + LANES), BF16 if chip else F32) for chip in chips),
                [vals, row_sums] + [resident(wi[chip * parts]) for chip in chips] + arrays,
                after=after,
                **product_cost(len(chips), 64),
            )

        early, late = (order[0], order[1]), (order[2], 0)
        sent_early = (early, for_others(early))
        sent_late = (late, for_others(late))
        (third,) = for_own(order[:1], [sent_early])
        first, second = for_own(order[1:], [sent_early, sent_late], third)
        arrived = across(third, order[0])
        far = [across(first, order[1]), across(second, order[2])]
        return for_own((0,), [sent_late], first, [arrived]) + tuple(far)

    taps_kept = tap_grads
    for step in range(sections):
        first, last = step == 0, step == sections - 1
        if not first:
            d_vals, taps_kept, sums = activation(step, upstream, taps_kept)
        terms = summed(d_vals, sums)
        block = SDS((rows, width), BF16)
        results = kernel_call(
            functools.partial(norm_kernel, model, first, last),
            SDS((rows + GAIN_ROWS, width), BF16) if last else (block, block, SDS((1, width), F32)),
            list(terms) + [normed, inv, gain, upstream] + ([] if first else [kept, gains, flags[step]]),
        )
        if last:
            own = results
        else:
            grad, kept, gains = results
            upstream = below(grad)

    far = {chip: across(own, chip) for chip in order}
    far[0] = own
    pieces = {
        (chip, side): sideways(far[chip], side) if side else far[chip]
        for chip in (0,) + order
        for side in range(parts)
    }
    early = [(0, side) for side in range(parts)] + [(order[0], 0)]
    late = [key for key in pieces if key not in early]
    results = []
    for keys in (early, late):
        results = kernel_call(
            functools.partial(
                assemble_kernel, seq, rows, [c * parts + side for c, side in keys], not results
            ),
            (SDS((2, seq, model), BF16), SDS((tensors, width), F32)),
            [full] + list(results) + [pieces[key] for key in keys],
            [
                pltpu.VMEM((seq - short, model), BF16),
                pltpu.SemaphoreType.DMA((2 * len(keys) + 1,)),
            ],
            specs=[VMEM] + ([HBM, VMEM] if results else []) + [VMEM] * len(keys),
            out_specs=(HBM, VMEM),
            aliases={1: 0, 2: 1} if results else {},
        )
    result, gain_grads = results[0], results[1].reshape(1, model)
    return (result[None], gain_grads, taps_kept[None])


def solution(mesh):
    placed = (
        P(),
        P(),
        P(),
        P("section", None, None, None),
        P("section", None, None, "tensor"),
        P("section", None),
        P("section", None, "tensor"),
        P("section", None, "tensor"),
        P("section", "tensor", None),
    )
    return jax.shard_map(
        local,
        mesh=mesh,
        in_specs=placed,
        out_specs=(
            P("section", None, None, None),
            P("section", None),
            P("section", None, "tensor"),
        ),
        check_vma=False,
    )
```

```python
import functools

import jax
import jax.numpy as jnp
from jax import lax
from jax.experimental import pallas as pl
from jax.experimental.pallas import tpu as pltpu
from jax.sharding import PartitionSpec as P

EPSILON = 1e-05
CHIPS = 4
LANES = 128
GAIN_ROWS = 8
F32 = jnp.float32
BF16 = jnp.bfloat16
NT = (((1,), (1,)), ((), ()))
NN = (((1,), (0,)), ((), ()))
VMEM = pl.BlockSpec(memory_space=pltpu.VMEM)
SMEM = pl.BlockSpec(memory_space=pltpu.SMEM)
HBM = pl.BlockSpec(memory_space=pltpu.HBM)
ANY = pl.BlockSpec(memory_space=pl.ANY)
MIB = 1 << 20
SDS = jax.ShapeDtypeStruct


def kernel_call(
    body, out_shape, operands, scratch=(), limit=4, flops=0, moved=0, specs=None, after=None, out_specs=None, aliases=None
):
    specs = specs or [SMEM if op.dtype == jnp.int32 else VMEM for op in operands]
    if after is not None:
        operands, specs = [after] + operands, [ANY] + specs
        body = functools.partial(skip_first, body)
    return pl.pallas_call(
        body,
        in_specs=specs,
        out_specs=out_specs
        or jax.tree.map(lambda _: VMEM, out_shape, is_leaf=lambda s: hasattr(s, "shape")),
        out_shape=out_shape,
        scratch_shapes=list(scratch),
        input_output_aliases=aliases or {},
        compiler_params=pltpu.CompilerParams(vmem_limit_bytes=limit * MIB),
        cost_estimate=pl.CostEstimate(flops=flops, bytes_accessed=moved, transcendentals=0),
    )(*operands)


def skip_first(body, _, *refs):
    body(*refs)


def resident(weights):
    return pltpu.with_memory_space_constraint(weights, pltpu.VMEM)


def moved_rows(values, by, seq):
    rows = values.shape[0]
    row = lax.broadcasted_iota(jnp.int32, values.shape, 0)
    if by > 0:
        keep = (row >= by) & ((row < seq) | (row >= seq + by))
        turned = pltpu.roll(values, by, 0)
    else:
        keep = (row < rows + by) & ((row < seq + by) | (row >= seq))
        turned = pltpu.roll(values, rows + by, 0)
    return jnp.where(keep, turned, 0.0)


def conv_backward(
    seq, acc_ref, slope_ref, rows_ref, taps_ref, inner_ref, vals_ref, grads_ref, active=None, kept_ref=None
):
    rows, channels = acc_ref.shape
    lags = taps_ref.shape[0]
    block = 256 if channels % 256 == 0 else LANES
    sums = jnp.zeros((rows, LANES), F32)

    def set_grads(lag, part, value):
        row = slice(lag, lag + 1)
        if kept_ref is not None:
            value = jnp.where(active, value, kept_ref[row, part])
        grads_ref[row, part] = value

    for at in range(0, channels, block):
        part = slice(at, at + block)
        d_pre = acc_ref[:, part] * slope_ref[:, part]
        values = rows_ref[:, part]
        d_vals = taps_ref[0:1, part] * d_pre
        set_grads(0, part, jnp.sum(d_pre * values, axis=0, keepdims=True))
        for lag in range(1, lags):
            ahead = moved_rows(d_pre, -lag, seq)
            d_vals = d_vals + taps_ref[lag : lag + 1, part] * ahead
            set_grads(lag, part, jnp.sum(ahead * values, axis=0, keepdims=True))
        rounded = d_vals.astype(BF16)
        vals_ref[:, part] = rounded
        product = rounded.astype(F32) * inner_ref[:, part]
        for lane in range(0, block, LANES):
            sums = sums + product[:, lane : lane + LANES]
    return jnp.broadcast_to(jnp.sum(sums, axis=1, keepdims=True), (rows, LANES))


def first_kernel(
    seq,
    me_slot,
    sections,
    idx_ref,
    counts_ref,
    *refs,
):
    sources, refs = refs[:6], refs[6:]
    wo_hbm, wi_hbm, *refs = refs
    vals_ref, grads_ref, sums_ref, inner_ref, slope_ref, rows_ref, *refs = refs
    normed_ref, inv_ref, up_ref, gain_part_ref, *refs = refs
    full_ref, *refs = refs
    flag_refs, refs = refs[:sections], refs[sections:]
    weights, refs = refs[:-10], refs[-10:]
    dy_ref, mask_ref, layer_ref, conv_ref, gain_ref, taps_ref, *refs = refs
    top_ref, scaled_ref, acc_ref, sem = refs
    blocks = len(weights) // 2
    wo_refs, wi_refs = weights[:blocks], weights[blocks:]
    model = gain_ref.shape[1]
    width = up_ref.shape[1]
    lags, channels = taps_ref.shape
    rows = acc_ref.shape[0]
    short = rows - seq

    def columns(i):
        return pl.ds(pl.multiple_of(idx_ref[me_slot + i] * width, width), width)

    held = [mask_ref, dy_ref, layer_ref, conv_ref, gain_ref, taps_ref]
    small = [
        pltpu.make_async_copy(source, ref, sem.at[2 * blocks + i])
        for i, (source, ref) in enumerate(zip(sources, held))
    ]
    out_copies = [
        pltpu.make_async_copy(wo_hbm.at[:, columns(i)], wo_refs[i], sem.at[i])
        for i in range(blocks)
    ]
    in_copies = [
        pltpu.make_async_copy(wi_hbm.at[columns(blocks + i), :], wi_refs[i], sem.at[blocks + i])
        for i in range(blocks)
    ]
    order = small[:2] + out_copies[:1] + small[2:]
    for i in range(blocks):
        order += in_copies[i : i + 1] + out_copies[i + 1 : i + 2]
    for copy in order:
        copy.start()

    for step, flag_ref in enumerate(flag_refs):
        flag = jnp.where(idx_ref[me_slot + 2 * blocks + step] == 1, 1.0, 0.0)
        flag_ref[...] = jnp.full(flag_ref.shape, flag, F32)
    full = jnp.where(counts_ref[0] == seq, 0, 1)
    full_ref[...] = jnp.full(full_ref.shape, jnp.where(full == 1, 1.0, 0.0), F32)

    def live(ref, part):
        head = ref[full, :, part].astype(F32)
        tail = ref[1 - full, :short, part].astype(F32)
        return jnp.concatenate([head, tail], axis=0)

    def keep_column(batch):
        lane = lax.broadcasted_iota(jnp.int32, (seq, seq), 1)
        row = lax.broadcasted_iota(jnp.int32, (seq, seq), 0)
        mask = jnp.broadcast_to(mask_ref[pl.ds(batch, 1), :], (seq, seq))
        on = (mask == 1) & (lane < counts_ref[batch]) & (lane == row)
        return jnp.sum(jnp.where(on, 1.0, 0.0), axis=1, keepdims=True)

    small[0].wait()
    keep = jnp.concatenate([keep_column(full), keep_column(1 - full)[:short]], axis=0)

    def make_top(i):
        top_ref[i] = (live(dy_ref, columns(i)) * keep).astype(BF16)

    block = 256 if channels % 256 == 0 else LANES
    slope_parts = list(range(0, channels, block))

    def make_slope(at):
        part = slice(at, at + block)
        values = live(conv_ref, part)
        rows_ref[:, part] = values
        pre_act = taps_ref[0:1, part] * values
        for lag in range(1, lags):
            pre_act = pre_act + taps_ref[lag : lag + 1, part] * moved_rows(values, lag, seq)
        gate = 1.0 / (1.0 + jnp.exp(-pre_act))
        slope_ref[:, part] = gate * (1.0 + pre_act * (1.0 - gate))

    def make_scaled(i):
        part = columns(blocks + i)
        scaled_ref[i % 2] = (live(layer_ref, part) * gain_ref[:, part]).astype(BF16)

    small[1].wait()
    make_top(0)
    up_ref[...] = top_ref[0]
    squares = jnp.zeros((rows, LANES), F32)
    for i in range(blocks):
        out_copies[i].wait()
        for at in range(0, channels, block):
            part = slice(at, at + block)
            term = lax.dot_general(top_ref[i], wo_refs[i][part, :], NT, preferred_element_type=F32)
            acc_ref[:, part] = term if i == 0 else acc_ref[:, part] + term
        if i == 0:
            for copy in small[2:]:
                copy.wait()
            make_scaled(0)
        if i + 1 < blocks:
            make_top(i + 1)
        values = live(layer_ref, slice(i * width, (i + 1) * width))
        values = values * values
        for lane in range(0, width, LANES):
            squares = squares + values[:, lane : lane + LANES]
        in_copies[i].wait()
        for at in range(0, channels, block):
            part = slice(at, at + block)
            term = lax.dot_general(
                scaled_ref[i % 2], wi_refs[i][:, part], NN, preferred_element_type=F32
            )
            inner_ref[:, part] = term if i == 0 else inner_ref[:, part] + term
        if i + 1 < blocks:
            make_scaled(i + 1)
        for at in slope_parts[i::blocks]:
            make_slope(at)
    mean = jnp.sum(squares, axis=1, keepdims=True) * (1.0 / model)
    inv = lax.rsqrt(mean + EPSILON)
    inv_ref[...] = jnp.broadcast_to(inv, inv_ref.shape)
    normed_ref[...] = live(layer_ref, columns(0)) * inv
    gain_part_ref[...] = gain_ref[:, columns(0)]
    for at in range(0, channels, block):
        part = slice(at, at + block)
        inner_ref[:, part] = inner_ref[:, part] * inv
    sums_ref[...] = conv_backward(
        seq, acc_ref, slope_ref, rows_ref, taps_ref, inner_ref, vals_ref, grads_ref
    )


def act_kernel(seq, count, first, last, *refs):
    pieces, wo_refs, refs = refs[:count], refs[count : 2 * count], refs[2 * count :]
    if not first:
        so_far, refs = refs[0], refs[1:]
    if last:
        slope_ref, rows_ref, taps_ref, inner_ref, kept_ref, working_ref, *refs = refs
        vals_ref, grads_ref, sums_ref, acc_ref = refs
    else:
        (acc_ref,) = refs
    channels = acc_ref.shape[1]
    block = 256 if channels % 256 == 0 else LANES
    for at in range(0, channels, block):
        part = slice(at, at + block)
        total = None if first else so_far[:, part]
        for piece, wo_ref in zip(pieces, wo_refs):
            term = lax.dot_general(piece[...], wo_ref[part, :], NT, preferred_element_type=F32)
            total = term if total is None else total + term
        acc_ref[:, part] = total
    if last:
        active = working_ref[0:1, 0:1] > 0.0
        sums_ref[...] = conv_backward(
            seq, acc_ref, slope_ref, rows_ref, taps_ref, inner_ref, vals_ref, grads_ref, active, kept_ref
        )


def block_product(vals_ref, wi_ref, at, chunk):
    return lax.dot_general(
        vals_ref[...], wi_ref[at : at + chunk, :], NT, preferred_element_type=F32
    )


def split_sums(sums):
    high = sums.astype(BF16)
    low = (sums - high.astype(F32)).astype(BF16)
    lane = lax.broadcasted_iota(jnp.int32, sums.shape, 1)
    return jnp.where(lane < LANES // 2, high.astype(F32), low.astype(F32)).astype(BF16)


def joined_sums(block, width):
    high = block[:, width : width + 1].astype(F32)
    return high + block[:, width + LANES // 2 : width + LANES // 2 + 1].astype(F32)


def other_blocks_kernel(vals_ref, sums_ref, *refs):
    wi_refs, out_ref = refs[:-1], refs[-1]
    width = out_ref.shape[2] - LANES
    chunk = min(512, width)
    for number, wi_ref in enumerate(wi_refs):
        for at in range(0, width, chunk):
            term = block_product(vals_ref, wi_ref, at, chunk)
            out_ref[number, :, at : at + chunk] = term.astype(BF16)
        out_ref[number, :, width:] = split_sums(sums_ref[...])


def own_blocks_kernel(chips, picks, vals_ref, sums_ref, *refs):
    count = len(chips)
    wi_refs, recv_refs, out_refs = refs[:count], refs[count:-count], refs[-count:]
    width = out_refs[0].shape[1] - LANES
    chunk = min(512, width)
    for chip, pick, wi_ref, out_ref in zip(chips, picks, wi_refs, out_refs):
        for at in range(0, width, chunk):
            term = block_product(vals_ref, wi_ref, at, chunk)
            for number, slot in pick:
                part = slice(at, at + chunk)
                recv = recv_refs[number]
                recv = recv[:, part] if slot is None else recv[slot, :, part]
                term = term + recv.astype(F32)
            out_ref[:, at : at + chunk] = term.astype(out_ref.dtype)
        sums = sums_ref[...]
        for number, slot in pick:
            recv = recv_refs[number]
            sums = sums + joined_sums(recv if slot is None else recv.at[slot], width)
        out_ref[:, width:] = split_sums(sums) if chip else sums


def norm_kernel(
    model,
    first,
    last,
    own_ref,
    a_ref,
    b_ref,
    normed_ref,
    inv_ref,
    gain_ref,
    up_ref,
    *refs,
):
    if not first:
        earlier_ref, gains_ref, working_ref, *refs = refs
        active = working_ref[0:1, 0:1] > 0.0
    if last:
        (out_ref,) = refs
    else:
        out_ref, kept_ref, sum_ref = refs
    rows, width = normed_ref.shape
    sums = own_ref[:, width : width + 1]
    for ref in (a_ref, b_ref):
        sums = sums + joined_sums(ref, width)
    mean = sums * (1.0 / model)
    inv = inv_ref[:, 0:1]
    chunk = min(512, width)
    for at in range(0, width, chunk):
        part = slice(at, at + chunk)
        d_norm = own_ref[:, part]
        for ref in (a_ref, b_ref):
            d_norm = d_norm + ref[:, part].astype(F32)
        normed = normed_ref[:, part]
        d_in = inv * (d_norm * gain_ref[:, part] - normed * mean)
        grad = up_ref[:, part].astype(F32) + d_in
        gains = jnp.sum(d_norm * normed, axis=0, keepdims=True)
        kept = grad
        if not first:
            kept = jnp.where(active, grad, earlier_ref[:, part].astype(F32))
            gains = jnp.where(active, gains, gains_ref[:, part])
        if last:
            high = gains.astype(BF16).astype(F32)
            row = lax.broadcasted_iota(jnp.int32, (GAIN_ROWS, chunk), 0)
            both = jnp.where(row == 0, high, jnp.where(row == 1, gains - high, 0.0))
            out_ref[:rows, part] = kept.astype(BF16)
            out_ref[rows:, part] = both.astype(BF16)
        else:
            out_ref[:, part] = grad.astype(BF16)
            kept_ref[:, part] = kept.astype(BF16)
            sum_ref[:, part] = gains


def assemble_kernel(seq, rows, distances, first, full_ref, *refs):
    if not first:
        refs = refs[2:]
    pieces, (out_ref, gain_ref, zero_ref, sem) = refs[:-4], refs[-4:]
    me = lax.axis_index("tensor")
    width = pieces[0].shape[1]
    full = jnp.where(jnp.max(full_ref[...]) > 0.5, 1, 0)
    short = rows - seq
    copies = []
    if first:
        zero_ref[...] = jnp.zeros(zero_ref.shape, BF16)
        copies.append(pltpu.make_async_copy(zero_ref, out_ref.at[1 - full, short:], sem.at[0]))
    for distance, piece in zip(distances, pieces):
        columns = pl.ds(pl.multiple_of((me ^ distance) * width, width), width)
        ends = (
            (piece.at[:seq], out_ref.at[full, :, columns]),
            (piece.at[seq:rows], out_ref.at[1 - full, :short, columns]),
        )
        for source, target in ends:
            copies.append(pltpu.make_async_copy(source, target, sem.at[len(copies)]))
    for copy in copies:
        copy.start()
    for distance, piece in zip(distances, pieces):
        gains = piece[rows:].astype(F32)
        gain_ref[pl.ds(me ^ distance, 1), :] = gains[0:1] + gains[1:2]
    for copy in copies:
        copy.wait()


def local(dy_top, loss_mask, counts, layer_in, conv_in, norm_gain, conv_weight, in_proj, out_proj):
    sections = lax.axis_size("section")
    tensors = lax.axis_size("tensor")
    section = lax.axis_index("section").astype(jnp.int32)
    me = lax.axis_index("tensor").astype(jnp.int32)
    seq, model = dy_top.shape[1:]
    short = seq // 2
    rows = seq + short
    parts = tensors // CHIPS
    width = model // tensors
    w_in, w_out, taps = in_proj[0], out_proj[0], conv_weight[0]
    lags, channels = taps.shape

    me_slot = 0

    blocks = jnp.arange(tensors, dtype=jnp.int32) ^ me
    roles = []
    for role in range(CHIPS):
        for side in range(parts):
            device = me ^ side
            odd = device & 1
            hop = {0: 0, 1: 1 + odd, 2: 2 - odd, 3: 3}[role]
            roles.append(device ^ (hop * parts))
    working = (jnp.arange(sections) == sections - 1 - section).astype(jnp.int32)
    table = jnp.concatenate([blocks, jnp.stack(roles), working])

    def across(x, chip):
        return lax.ppermute(x, "tensor", [(i, i ^ (chip * parts)) for i in range(tensors)])

    def first_hop(x):
        pairs = [(i, i ^ (2 * parts if i % 2 else parts)) for i in range(tensors)]
        return lax.ppermute(x, "tensor", pairs)

    def second_hop(x):
        pairs = [(i, i ^ (parts if i % 2 else 2 * parts)) for i in range(tensors)]
        return lax.ppermute(x, "tensor", pairs)

    def sideways(x, side):
        return lax.ppermute(x, "tensor", [(i, i ^ side) for i in range(tensors)])

    def below(x):
        return lax.ppermute(x, "section", [(i, i - 1) for i in range(1, sections)])

    sides = range(1, parts)
    order = (3, 1, 2)

    def product_cost(count, as_rows=512):
        return dict(
            flops=2 * as_rows * channels * width * count,
            moved=2 * channels * width * count,
        )

    vals_shape = SDS((rows, channels), BF16)
    grads_shape = SDS((lags, channels), F32)
    sums_shape = SDS((rows, LANES), F32)
    channel_shape = SDS((rows, channels), F32)
    block_rows = [(channels, width)] * tensors + [(width, channels)] * tensors
    d_vals, tap_grads, sums, inner, slope, conv_rows, normed, inv, upstream, gain, *rest = kernel_call(
        functools.partial(first_kernel, seq, me_slot, sections),
        (
            vals_shape,
            grads_shape,
            sums_shape,
            channel_shape,
            channel_shape,
            channel_shape,
            SDS((rows, width), F32),
            SDS((rows, LANES), F32),
            SDS((rows, width), BF16),
            SDS((1, width), F32),
        )
        + (SDS((8, LANES), F32),) * (1 + sections)
        + tuple(pltpu.VMEM(shape, BF16) for shape in block_rows),
        [table, counts]
        + [
            pltpu.with_memory_space_constraint(source, pltpu.HBM)
            for source in (
                loss_mask, dy_top, layer_in[0], conv_in[0], norm_gain, taps, w_out, w_in
            )
        ],
        [
            pltpu.VMEM(dy_top.shape, BF16),
            pltpu.VMEM(loss_mask.shape, jnp.int32),
            pltpu.VMEM(layer_in.shape[1:], BF16),
            pltpu.VMEM(conv_in.shape[1:], BF16),
            pltpu.VMEM(norm_gain.shape, F32),
            pltpu.VMEM(taps.shape, F32),
            pltpu.VMEM((tensors, rows, width), BF16),
            pltpu.VMEM((2, rows, width), BF16),
            pltpu.VMEM((rows, channels), F32),
            pltpu.SemaphoreType.DMA((2 * tensors + 6,)),
        ],
        limit=12,
        flops=4 * rows * channels * model,
        moved=4 * channels * model,
        specs=[SMEM, SMEM] + [HBM] * 8,
    )
    full, *rest = rest
    flags, weights = rest[:sections], rest[sections:]
    wo, wi = weights[:tensors], weights[tensors:]

    def activation(step, own, taps_kept):
        far = {chip: across(own, chip) for chip in order}
        far[0] = own
        plan = (0,) + order
        total, waiting = None, []
        for number in range(len(plan) + 1):
            first, last = number == 0, number == len(plan)
            group, waiting = waiting, []
            if not last:
                chip = plan[number]
                piece = far[chip]
                if not first:
                    piece, total = lax.optimization_barrier((piece, total))
                group.append((piece, chip, 0))
                waiting = [(sideways(piece, side), chip, side) for side in sides]
            operands = [piece for piece, _, _ in group]
            operands += [resident(wo[chip * parts + side]) for _, chip, side in group]
            operands += [] if first else [total]
            operands += [slope, conv_rows, taps, inner, taps_kept, flags[step]] if last else []
            total = kernel_call(
                functools.partial(act_kernel, seq, len(group), first, last),
                (vals_shape, grads_shape, sums_shape) if last else channel_shape,
                operands,
                [pltpu.VMEM((rows, channels), F32)] if last else [],
                **product_cost(len(group), 512),
            )
        return total

    def summed(vals, row_sums):
        def for_others(chips):
            return [
                sideways(
                    kernel_call(
                        other_blocks_kernel,
                        SDS((len(chips), rows, width + LANES), BF16),
                        [vals, row_sums] + [resident(wi[chip * parts + side]) for chip in chips],
                        **product_cost(len(chips), 64),
                    ),
                    side,
                )
                for side in sides
            ]

        def for_own(chips, batches, after=None, arrays=()):
            arrays = list(arrays)
            picks = [[(number, None) for number in range(len(arrays))] for _ in chips]
            for batch_chips, batch in batches:
                for array in batch:
                    for slot, chip in enumerate(batch_chips):
                        if chip in chips:
                            picks[chips.index(chip)].append((len(arrays), slot))
                    arrays.append(array)
            return kernel_call(
                functools.partial(own_blocks_kernel, chips, picks),
                tuple(SDS((rows, width + LANES), BF16 if chip else F32) for chip in chips),
                [vals, row_sums] + [resident(wi[chip * parts]) for chip in chips] + arrays,
                after=after,
                **product_cost(len(chips), 64),
            )

        early, late = (order[0], order[1]), (order[2], 0)
        sent_early = (early, for_others(early))
        sent_late = (late, for_others(late))
        (third,) = for_own(order[:1], [sent_early])
        passing = first_hop(third)
        (first,) = for_own(order[1:2], [sent_early], third)
        (second,) = for_own(order[2:], [sent_late], first, [passing])
        (own,) = for_own((0,), [sent_late], second)
        return own, first_hop(first), second_hop(second)

    taps_kept = tap_grads
    for step in range(sections):
        first, last = step == 0, step == sections - 1
        if not first:
            d_vals, taps_kept, sums = activation(step, upstream, taps_kept)
        terms = summed(d_vals, sums)
        block = SDS((rows, width), BF16)
        results = kernel_call(
            functools.partial(norm_kernel, model, first, last),
            SDS((rows + GAIN_ROWS, width), BF16) if last else (block, block, SDS((1, width), F32)),
            list(terms) + [normed, inv, gain, upstream] + ([] if first else [kept, gains, flags[step]]),
        )
        if last:
            own = results
        else:
            grad, kept, gains = results
            upstream = below(grad)

    far = {chip: across(own, chip) for chip in order}
    far[0] = own
    pieces = {
        (chip, side): sideways(far[chip], side) if side else far[chip]
        for chip in (0,) + order
        for side in range(parts)
    }
    early = [(0, side) for side in range(parts)] + [(order[0], 0)]
    late = [key for key in pieces if key not in early]
    results = []
    for keys in (early, late):
        results = kernel_call(
            functools.partial(
                assemble_kernel, seq, rows, [c * parts + side for c, side in keys], not results
            ),
            (SDS((2, seq, model), BF16), SDS((tensors, width), F32)),
            [full] + list(results) + [pieces[key] for key in keys],
            [
                pltpu.VMEM((seq - short, model), BF16),
                pltpu.SemaphoreType.DMA((2 * len(keys) + 1,)),
            ],
            specs=[VMEM] + ([HBM, VMEM] if results else []) + [VMEM] * len(keys),
            out_specs=(HBM, VMEM),
            aliases={1: 0, 2: 1} if results else {},
        )
    result, gain_grads = results[0], results[1].reshape(1, model)
    return (result[None], gain_grads, taps_kept[None])


def solution(mesh):
    placed = (
        P(),
        P(),
        P(),
        P("section", None, None, None),
        P("section", None, None, "tensor"),
        P("section", None),
        P("section", None, "tensor"),
        P("section", None, "tensor"),
        P("section", "tensor", None),
    )
    return jax.shard_map(
        local,
        mesh=mesh,
        in_specs=placed,
        out_specs=(
            P("section", None, None, None),
            P("section", None),
            P("section", None, "tensor"),
        ),
        check_vma=False,
    )
```

```python
import functools

import jax
import jax.numpy as jnp
from jax import lax
from jax.experimental import pallas as pl
from jax.experimental.pallas import tpu as pltpu
from jax.sharding import PartitionSpec as P

EPSILON = 1e-05
CHIPS = 4
LANES = 128
GAIN_ROWS = 8
F32 = jnp.float32
BF16 = jnp.bfloat16
NT = (((1,), (1,)), ((), ()))
NN = (((1,), (0,)), ((), ()))
VMEM = pl.BlockSpec(memory_space=pltpu.VMEM)
SMEM = pl.BlockSpec(memory_space=pltpu.SMEM)
HBM = pl.BlockSpec(memory_space=pltpu.HBM)
ANY = pl.BlockSpec(memory_space=pl.ANY)
MIB = 1 << 20
SDS = jax.ShapeDtypeStruct


def kernel_call(
    body, out_shape, operands, scratch=(), limit=4, flops=0, moved=0, specs=None, after=None, out_specs=None, aliases=None
):
    specs = specs or [SMEM if op.dtype == jnp.int32 else VMEM for op in operands]
    if after is not None:
        operands, specs = [after] + operands, [ANY] + specs
        body = functools.partial(skip_first, body)
    return pl.pallas_call(
        body,
        in_specs=specs,
        out_specs=out_specs
        or jax.tree.map(lambda _: VMEM, out_shape, is_leaf=lambda s: hasattr(s, "shape")),
        out_shape=out_shape,
        scratch_shapes=list(scratch),
        input_output_aliases=aliases or {},
        compiler_params=pltpu.CompilerParams(vmem_limit_bytes=limit * MIB),
        cost_estimate=pl.CostEstimate(flops=flops, bytes_accessed=moved, transcendentals=0),
    )(*operands)


def skip_first(body, _, *refs):
    body(*refs)


def resident(weights):
    return pltpu.with_memory_space_constraint(weights, pltpu.VMEM)


def moved_rows(values, by, seq):
    rows = values.shape[0]
    row = lax.broadcasted_iota(jnp.int32, values.shape, 0)
    if by > 0:
        keep = (row >= by) & ((row < seq) | (row >= seq + by))
        turned = pltpu.roll(values, by, 0)
    else:
        keep = (row < rows + by) & ((row < seq + by) | (row >= seq))
        turned = pltpu.roll(values, rows + by, 0)
    return jnp.where(keep, turned, 0.0)


def conv_backward(
    seq, acc_ref, slope_ref, rows_ref, taps_ref, inner_ref, vals_ref, grads_ref, active=None, kept_ref=None
):
    rows, channels = acc_ref.shape
    lags = taps_ref.shape[0]
    block = 256 if channels % 256 == 0 else LANES
    sums = jnp.zeros((rows, LANES), F32)

    def set_grads(lag, part, value):
        row = slice(lag, lag + 1)
        if kept_ref is not None:
            value = jnp.where(active, value, kept_ref[row, part])
        grads_ref[row, part] = value

    for at in range(0, channels, block):
        part = slice(at, at + block)
        d_pre = acc_ref[:, part] * slope_ref[:, part]
        values = rows_ref[:, part]
        d_vals = taps_ref[0:1, part] * d_pre
        set_grads(0, part, jnp.sum(d_pre * values, axis=0, keepdims=True))
        for lag in range(1, lags):
            ahead = moved_rows(d_pre, -lag, seq)
            d_vals = d_vals + taps_ref[lag : lag + 1, part] * ahead
            set_grads(lag, part, jnp.sum(ahead * values, axis=0, keepdims=True))
        rounded = d_vals.astype(BF16)
        vals_ref[:, part] = rounded
        product = rounded.astype(F32) * inner_ref[:, part]
        for lane in range(0, block, LANES):
            sums = sums + product[:, lane : lane + LANES]
    return jnp.broadcast_to(jnp.sum(sums, axis=1, keepdims=True), (rows, LANES))


def first_kernel(
    seq,
    me_slot,
    sections,
    idx_ref,
    *refs,
):
    sources, refs = refs[:7], refs[7:]
    wo_hbm, wi_hbm, *refs = refs
    vals_ref, grads_ref, sums_ref, inner_ref, slope_ref, rows_ref, *refs = refs
    normed_ref, inv_ref, up_ref, gain_part_ref, *refs = refs
    full_ref, *refs = refs
    flag_refs, refs = refs[:sections], refs[sections:]
    weights, refs = refs[:-11], refs[-11:]
    counts_ref, dy_ref, mask_ref, layer_ref, conv_ref, gain_ref, taps_ref, *refs = refs
    top_ref, scaled_ref, acc_ref, sem = refs
    blocks = len(weights) // 2
    wo_refs, wi_refs = weights[:blocks], weights[blocks:]
    model = gain_ref.shape[1]
    width = up_ref.shape[1]
    lags, channels = taps_ref.shape
    rows = acc_ref.shape[0]
    short = rows - seq

    def columns(i):
        return pl.ds(pl.multiple_of(idx_ref[me_slot + i] * width, width), width)

    held = [counts_ref, mask_ref, dy_ref, layer_ref, conv_ref, gain_ref, taps_ref]
    small = [
        pltpu.make_async_copy(source, ref, sem.at[2 * blocks + i])
        for i, (source, ref) in enumerate(zip(sources, held))
    ]
    out_copies = [
        pltpu.make_async_copy(wo_hbm.at[:, columns(i)], wo_refs[i], sem.at[i])
        for i in range(blocks)
    ]
    in_copies = [
        pltpu.make_async_copy(wi_hbm.at[columns(blocks + i), :], wi_refs[i], sem.at[blocks + i])
        for i in range(blocks)
    ]
    order = small[:3] + out_copies[:1] + small[3:]
    for i in range(blocks):
        order += in_copies[i : i + 1] + out_copies[i + 1 : i + 2]
    for copy in order:
        copy.start()

    for step, flag_ref in enumerate(flag_refs):
        flag = jnp.where(idx_ref[me_slot + 2 * blocks + step] == 1, 1.0, 0.0)
        flag_ref[...] = jnp.full(flag_ref.shape, flag, F32)
    small[0].wait()
    full = jnp.where(counts_ref[0] == seq, 0, 1)
    full_ref[...] = jnp.full(full_ref.shape, jnp.where(full == 1, 1.0, 0.0), F32)

    def live(ref, part):
        head = ref[full, :, part].astype(F32)
        tail = ref[1 - full, :short, part].astype(F32)
        return jnp.concatenate([head, tail], axis=0)

    def keep_column(batch):
        lane = lax.broadcasted_iota(jnp.int32, (seq, seq), 1)
        row = lax.broadcasted_iota(jnp.int32, (seq, seq), 0)
        mask = jnp.broadcast_to(mask_ref[pl.ds(batch, 1), :], (seq, seq))
        on = (mask == 1) & (lane < counts_ref[batch]) & (lane == row)
        return jnp.sum(jnp.where(on, 1.0, 0.0), axis=1, keepdims=True)

    small[1].wait()
    keep = jnp.concatenate([keep_column(full), keep_column(1 - full)[:short]], axis=0)

    def make_top(i):
        top_ref[i] = (live(dy_ref, columns(i)) * keep).astype(BF16)

    block = 256 if channels % 256 == 0 else LANES
    slope_parts = list(range(0, channels, block))

    def make_slope(at):
        part = slice(at, at + block)
        values = live(conv_ref, part)
        rows_ref[:, part] = values
        pre_act = taps_ref[0:1, part] * values
        for lag in range(1, lags):
            pre_act = pre_act + taps_ref[lag : lag + 1, part] * moved_rows(values, lag, seq)
        gate = 1.0 / (1.0 + jnp.exp(-pre_act))
        slope_ref[:, part] = gate * (1.0 + pre_act * (1.0 - gate))

    def make_scaled(i):
        part = columns(blocks + i)
        scaled_ref[i % 2] = (live(layer_ref, part) * gain_ref[:, part]).astype(BF16)

    small[2].wait()
    make_top(0)
    up_ref[...] = top_ref[0]
    squares = jnp.zeros((rows, LANES), F32)
    for i in range(blocks):
        out_copies[i].wait()
        for at in range(0, channels, block):
            part = slice(at, at + block)
            term = lax.dot_general(top_ref[i], wo_refs[i][part, :], NT, preferred_element_type=F32)
            acc_ref[:, part] = term if i == 0 else acc_ref[:, part] + term
        if i == 0:
            for copy in small[3:]:
                copy.wait()
            make_scaled(0)
        if i + 1 < blocks:
            make_top(i + 1)
        values = live(layer_ref, slice(i * width, (i + 1) * width))
        values = values * values
        for lane in range(0, width, LANES):
            squares = squares + values[:, lane : lane + LANES]
        in_copies[i].wait()
        for at in range(0, channels, block):
            part = slice(at, at + block)
            term = lax.dot_general(
                scaled_ref[i % 2], wi_refs[i][:, part], NN, preferred_element_type=F32
            )
            inner_ref[:, part] = term if i == 0 else inner_ref[:, part] + term
        if i + 1 < blocks:
            make_scaled(i + 1)
        for at in slope_parts[i::blocks]:
            make_slope(at)
    mean = jnp.sum(squares, axis=1, keepdims=True) * (1.0 / model)
    inv = lax.rsqrt(mean + EPSILON)
    inv_ref[...] = jnp.broadcast_to(inv, inv_ref.shape)
    normed_ref[...] = live(layer_ref, columns(0)) * inv
    gain_part_ref[...] = gain_ref[:, columns(0)]
    for at in range(0, channels, block):
        part = slice(at, at + block)
        inner_ref[:, part] = inner_ref[:, part] * inv
    sums_ref[...] = conv_backward(
        seq, acc_ref, slope_ref, rows_ref, taps_ref, inner_ref, vals_ref, grads_ref
    )


def act_kernel(seq, count, first, last, *refs):
    pieces, wo_refs, refs = refs[:count], refs[count : 2 * count], refs[2 * count :]
    if not first:
        so_far, refs = refs[0], refs[1:]
    if last:
        slope_ref, rows_ref, taps_ref, inner_ref, kept_ref, working_ref, *refs = refs
        vals_ref, grads_ref, sums_ref, acc_ref = refs
    else:
        (acc_ref,) = refs
    channels = acc_ref.shape[1]
    block = 256 if channels % 256 == 0 else LANES
    for at in range(0, channels, block):
        part = slice(at, at + block)
        total = None if first else so_far[:, part]
        for piece, wo_ref in zip(pieces, wo_refs):
            term = lax.dot_general(piece[...], wo_ref[part, :], NT, preferred_element_type=F32)
            total = term if total is None else total + term
        acc_ref[:, part] = total
    if last:
        active = working_ref[0:1, 0:1] > 0.0
        sums_ref[...] = conv_backward(
            seq, acc_ref, slope_ref, rows_ref, taps_ref, inner_ref, vals_ref, grads_ref, active, kept_ref
        )


def block_product(vals_ref, wi_ref, at, chunk):
    return lax.dot_general(
        vals_ref[...], wi_ref[at : at + chunk, :], NT, preferred_element_type=F32
    )


def split_sums(sums):
    high = sums.astype(BF16)
    low = (sums - high.astype(F32)).astype(BF16)
    lane = lax.broadcasted_iota(jnp.int32, sums.shape, 1)
    return jnp.where(lane < LANES // 2, high.astype(F32), low.astype(F32)).astype(BF16)


def joined_sums(block, width):
    high = block[:, width : width + 1].astype(F32)
    return high + block[:, width + LANES // 2 : width + LANES // 2 + 1].astype(F32)


def other_blocks_kernel(vals_ref, sums_ref, *refs):
    wi_refs, out_ref = refs[:-1], refs[-1]
    width = out_ref.shape[2] - LANES
    chunk = min(512, width)
    for number, wi_ref in enumerate(wi_refs):
        for at in range(0, width, chunk):
            term = block_product(vals_ref, wi_ref, at, chunk)
            out_ref[number, :, at : at + chunk] = term.astype(BF16)
        out_ref[number, :, width:] = split_sums(sums_ref[...])


def own_blocks_kernel(chips, picks, vals_ref, sums_ref, *refs):
    count = len(chips)
    wi_refs, recv_refs, out_refs = refs[:count], refs[count:-count], refs[-count:]
    width = out_refs[0].shape[1] - LANES
    chunk = min(512, width)
    for chip, pick, wi_ref, out_ref in zip(chips, picks, wi_refs, out_refs):
        for at in range(0, width, chunk):
            term = block_product(vals_ref, wi_ref, at, chunk)
            for number, slot in pick:
                part = slice(at, at + chunk)
                recv = recv_refs[number]
                recv = recv[:, part] if slot is None else recv[slot, :, part]
                term = term + recv.astype(F32)
            out_ref[:, at : at + chunk] = term.astype(out_ref.dtype)
        sums = sums_ref[...]
        for number, slot in pick:
            recv = recv_refs[number]
            sums = sums + joined_sums(recv if slot is None else recv.at[slot], width)
        out_ref[:, width:] = split_sums(sums) if chip else sums


def norm_kernel(
    model,
    first,
    last,
    own_ref,
    a_ref,
    b_ref,
    normed_ref,
    inv_ref,
    gain_ref,
    up_ref,
    *refs,
):
    if not first:
        earlier_ref, gains_ref, working_ref, *refs = refs
        active = working_ref[0:1, 0:1] > 0.0
    if last:
        (out_ref,) = refs
    else:
        out_ref, kept_ref, sum_ref = refs
    rows, width = normed_ref.shape
    sums = own_ref[:, width : width + 1]
    for ref in (a_ref, b_ref):
        sums = sums + joined_sums(ref, width)
    mean = sums * (1.0 / model)
    inv = inv_ref[:, 0:1]
    chunk = min(512, width)
    for at in range(0, width, chunk):
        part = slice(at, at + chunk)
        d_norm = own_ref[:, part]
        for ref in (a_ref, b_ref):
            d_norm = d_norm + ref[:, part].astype(F32)
        normed = normed_ref[:, part]
        d_in = inv * (d_norm * gain_ref[:, part] - normed * mean)
        grad = up_ref[:, part].astype(F32) + d_in
        gains = jnp.sum(d_norm * normed, axis=0, keepdims=True)
        kept = grad
        if not first:
            kept = jnp.where(active, grad, earlier_ref[:, part].astype(F32))
            gains = jnp.where(active, gains, gains_ref[:, part])
        if last:
            high = gains.astype(BF16).astype(F32)
            row = lax.broadcasted_iota(jnp.int32, (GAIN_ROWS, chunk), 0)
            both = jnp.where(row == 0, high, jnp.where(row == 1, gains - high, 0.0))
            out_ref[:rows, part] = kept.astype(BF16)
            out_ref[rows:, part] = both.astype(BF16)
        else:
            out_ref[:, part] = grad.astype(BF16)
            kept_ref[:, part] = kept.astype(BF16)
            sum_ref[:, part] = gains


def assemble_kernel(seq, rows, distances, first, full_ref, *refs):
    if not first:
        refs = refs[2:]
    pieces, (out_ref, gain_ref, zero_ref, sem) = refs[:-4], refs[-4:]
    me = lax.axis_index("tensor")
    width = pieces[0].shape[1]
    full = jnp.where(jnp.max(full_ref[...]) > 0.5, 1, 0)
    short = rows - seq
    copies = []
    if first:
        zero_ref[...] = jnp.zeros(zero_ref.shape, BF16)
        copies.append(pltpu.make_async_copy(zero_ref, out_ref.at[1 - full, short:], sem.at[0]))
    for distance, piece in zip(distances, pieces):
        columns = pl.ds(pl.multiple_of((me ^ distance) * width, width), width)
        ends = (
            (piece.at[:seq], out_ref.at[full, :, columns]),
            (piece.at[seq:rows], out_ref.at[1 - full, :short, columns]),
        )
        for source, target in ends:
            copies.append(pltpu.make_async_copy(source, target, sem.at[len(copies)]))
    for copy in copies:
        copy.start()
    for distance, piece in zip(distances, pieces):
        gains = piece[rows:].astype(F32)
        gain_ref[pl.ds(me ^ distance, 1), :] = gains[0:1] + gains[1:2]
    for copy in copies:
        copy.wait()


def local(dy_top, loss_mask, counts, layer_in, conv_in, norm_gain, conv_weight, in_proj, out_proj):
    sections = lax.axis_size("section")
    tensors = lax.axis_size("tensor")
    section = lax.axis_index("section").astype(jnp.int32)
    me = lax.axis_index("tensor").astype(jnp.int32)
    seq, model = dy_top.shape[1:]
    short = seq // 2
    rows = seq + short
    parts = tensors // CHIPS
    width = model // tensors
    w_in, w_out, taps = in_proj[0], out_proj[0], conv_weight[0]
    lags, channels = taps.shape

    me_slot = 0

    blocks = jnp.arange(tensors, dtype=jnp.int32) ^ me
    roles = []
    for role in range(CHIPS):
        for side in range(parts):
            device = me ^ side
            odd = device & 1
            hop = {0: 0, 1: 1 + odd, 2: 2 - odd, 3: 3}[role]
            roles.append(device ^ (hop * parts))
    working = (jnp.arange(sections) == sections - 1 - section).astype(jnp.int32)
    table = jnp.concatenate([blocks, jnp.stack(roles), working])

    def across(x, chip):
        return lax.ppermute(x, "tensor", [(i, i ^ (chip * parts)) for i in range(tensors)])

    def first_hop(x):
        pairs = [(i, i ^ (2 * parts if i % 2 else parts)) for i in range(tensors)]
        return lax.ppermute(x, "tensor", pairs)

    def second_hop(x):
        pairs = [(i, i ^ (parts if i % 2 else 2 * parts)) for i in range(tensors)]
        return lax.ppermute(x, "tensor", pairs)

    def sideways(x, side):
        return lax.ppermute(x, "tensor", [(i, i ^ side) for i in range(tensors)])

    def below(x):
        return lax.ppermute(x, "section", [(i, i - 1) for i in range(1, sections)])

    sides = range(1, parts)
    order = (3, 1, 2)

    def product_cost(count, as_rows=512):
        return dict(
            flops=2 * as_rows * channels * width * count,
            moved=2 * channels * width * count,
        )

    vals_shape = SDS((rows, channels), BF16)
    grads_shape = SDS((lags, channels), F32)
    sums_shape = SDS((rows, LANES), F32)
    channel_shape = SDS((rows, channels), F32)
    block_rows = [(channels, width)] * tensors + [(width, channels)] * tensors
    d_vals, tap_grads, sums, inner, slope, conv_rows, normed, inv, upstream, gain, *rest = kernel_call(
        functools.partial(first_kernel, seq, me_slot, sections),
        (
            vals_shape,
            grads_shape,
            sums_shape,
            channel_shape,
            channel_shape,
            channel_shape,
            SDS((rows, width), F32),
            SDS((rows, LANES), F32),
            SDS((rows, width), BF16),
            SDS((1, width), F32),
        )
        + (SDS((8, LANES), F32),) * (1 + sections)
        + tuple(pltpu.VMEM(shape, BF16) for shape in block_rows),
        [table]
        + [
            pltpu.with_memory_space_constraint(source, pltpu.HBM)
            for source in (
                counts, loss_mask, dy_top, layer_in[0], conv_in[0], norm_gain, taps, w_out, w_in
            )
        ],
        [
            pltpu.SMEM(counts.shape, jnp.int32),
            pltpu.VMEM(dy_top.shape, BF16),
            pltpu.VMEM(loss_mask.shape, jnp.int32),
            pltpu.VMEM(layer_in.shape[1:], BF16),
            pltpu.VMEM(conv_in.shape[1:], BF16),
            pltpu.VMEM(norm_gain.shape, F32),
            pltpu.VMEM(taps.shape, F32),
            pltpu.VMEM((tensors, rows, width), BF16),
            pltpu.VMEM((2, rows, width), BF16),
            pltpu.VMEM((rows, channels), F32),
            pltpu.SemaphoreType.DMA((2 * tensors + 7,)),
        ],
        limit=12,
        flops=4 * rows * channels * model,
        moved=4 * channels * model,
        specs=[SMEM] + [HBM] * 9,
    )
    full, *rest = rest
    flags, weights = rest[:sections], rest[sections:]
    wo, wi = weights[:tensors], weights[tensors:]

    def activation(step, own, taps_kept):
        far = {chip: across(own, chip) for chip in order}
        far[0] = own
        plan = (0,) + order
        total, waiting = None, []
        for number in range(len(plan) + 1):
            first, last = number == 0, number == len(plan)
            group, waiting = waiting, []
            if not last:
                chip = plan[number]
                piece = far[chip]
                if not first:
                    piece, total = lax.optimization_barrier((piece, total))
                group.append((piece, chip, 0))
                waiting = [(sideways(piece, side), chip, side) for side in sides]
            operands = [piece for piece, _, _ in group]
            operands += [resident(wo[chip * parts + side]) for _, chip, side in group]
            operands += [] if first else [total]
            operands += [slope, conv_rows, taps, inner, taps_kept, flags[step]] if last else []
            total = kernel_call(
                functools.partial(act_kernel, seq, len(group), first, last),
                (vals_shape, grads_shape, sums_shape) if last else channel_shape,
                operands,
                [pltpu.VMEM((rows, channels), F32)] if last else [],
                **product_cost(len(group), 512),
            )
        return total

    def summed(vals, row_sums):
        def for_others(chips, after=None):
            return [
                sideways(
                    kernel_call(
                        other_blocks_kernel,
                        SDS((len(chips), rows, width + LANES), BF16),
                        [vals, row_sums] + [resident(wi[chip * parts + side]) for chip in chips],
                        after=after,
                        **product_cost(len(chips), 64),
                    ),
                    side,
                )
                for side in sides
            ]

        def for_own(chips, batches, after=None, arrays=()):
            arrays = list(arrays)
            picks = [[(number, None) for number in range(len(arrays))] for _ in chips]
            for batch_chips, batch in batches:
                for array in batch:
                    for slot, chip in enumerate(batch_chips):
                        if chip in chips:
                            picks[chips.index(chip)].append((len(arrays), slot))
                    arrays.append(array)
            return kernel_call(
                functools.partial(own_blocks_kernel, chips, picks),
                tuple(SDS((rows, width + LANES), BF16 if chip else F32) for chip in chips),
                [vals, row_sums] + [resident(wi[chip * parts]) for chip in chips] + arrays,
                after=after,
                **product_cost(len(chips), 64),
            )

        early, late = (order[0], order[1]), order[2:]
        sent_early = (early, for_others(early))
        sent_late = (late, for_others(late))
        (third,) = for_own(order[:1], [sent_early])
        passing = first_hop(third)
        (first,) = for_own(order[1:2], [sent_early], third)
        (second,) = for_own(order[2:], [sent_late], first, [passing])
        (own,) = for_own((0,), [((0,), for_others((0,), first))], second)
        return own, first_hop(first), second_hop(second)

    taps_kept = tap_grads
    for step in range(sections):
        first, last = step == 0, step == sections - 1
        if not first:
            d_vals, taps_kept, sums = activation(step, upstream, taps_kept)
        terms = summed(d_vals, sums)
        block = SDS((rows, width), BF16)
        results = kernel_call(
            functools.partial(norm_kernel, model, first, last),
            SDS((rows + GAIN_ROWS, width), BF16) if last else (block, block, SDS((1, width), F32)),
            list(terms) + [normed, inv, gain, upstream] + ([] if first else [kept, gains, flags[step]]),
        )
        if last:
            own = results
        else:
            grad, kept, gains = results
            upstream = below(grad)

    far = {chip: across(own, chip) for chip in order}
    far[0] = own
    pieces = {
        (chip, side): sideways(far[chip], side) if side else far[chip]
        for chip in (0,) + order
        for side in range(parts)
    }
    early = [(0, side) for side in range(parts)] + [(order[0], 0)]
    late = [key for key in pieces if key not in early]
    results = []
    for keys in (early, late):
        results = kernel_call(
            functools.partial(
                assemble_kernel, seq, rows, [c * parts + side for c, side in keys], not results
            ),
            (SDS((2, seq, model), BF16), SDS((tensors, width), F32)),
            [full] + list(results) + [pieces[key] for key in keys],
            [
                pltpu.VMEM((seq - short, model), BF16),
                pltpu.SemaphoreType.DMA((2 * len(keys) + 1,)),
            ],
            specs=[VMEM] + ([HBM, VMEM] if results else []) + [VMEM] * len(keys),
            out_specs=(HBM, VMEM),
            aliases={1: 0, 2: 1} if results else {},
        )
    result, gain_grads = results[0], results[1].reshape(1, model)
    return (result[None], gain_grads, taps_kept[None])


def solution(mesh):
    placed = (
        P(),
        P(),
        P(),
        P("section", None, None, None),
        P("section", None, None, "tensor"),
        P("section", None),
        P("section", None, "tensor"),
        P("section", None, "tensor"),
        P("section", "tensor", None),
    )
    return jax.shard_map(
        local,
        mesh=mesh,
        in_specs=placed,
        out_specs=(
            P("section", None, None, None),
            P("section", None),
            P("section", None, "tensor"),
        ),
        check_vma=False,
    )
```

```python
import functools

import jax
import jax.numpy as jnp
from jax import lax
from jax.experimental import pallas as pl
from jax.experimental.pallas import tpu as pltpu
from jax.sharding import PartitionSpec as P

EPSILON = 1e-05
CHIPS = 4
LANES = 128
GAIN_ROWS = 8
F32 = jnp.float32
BF16 = jnp.bfloat16
NT = (((1,), (1,)), ((), ()))
NN = (((1,), (0,)), ((), ()))
VMEM = pl.BlockSpec(memory_space=pltpu.VMEM)
SMEM = pl.BlockSpec(memory_space=pltpu.SMEM)
HBM = pl.BlockSpec(memory_space=pltpu.HBM)
ANY = pl.BlockSpec(memory_space=pl.ANY)
MIB = 1 << 20
SDS = jax.ShapeDtypeStruct


def kernel_call(
    body, out_shape, operands, scratch=(), limit=4, flops=0, moved=0, specs=None, after=None, out_specs=None, aliases=None
):
    specs = specs or [SMEM if op.dtype == jnp.int32 else VMEM for op in operands]
    if after is not None:
        operands, specs = [after] + operands, [ANY] + specs
        body = functools.partial(skip_first, body)
    return pl.pallas_call(
        body,
        in_specs=specs,
        out_specs=out_specs
        or jax.tree.map(lambda _: VMEM, out_shape, is_leaf=lambda s: hasattr(s, "shape")),
        out_shape=out_shape,
        scratch_shapes=list(scratch),
        input_output_aliases=aliases or {},
        compiler_params=pltpu.CompilerParams(vmem_limit_bytes=limit * MIB),
        cost_estimate=pl.CostEstimate(flops=flops, bytes_accessed=moved, transcendentals=0),
    )(*operands)


def skip_first(body, _, *refs):
    body(*refs)


def resident(weights):
    return pltpu.with_memory_space_constraint(weights, pltpu.VMEM)


def moved_rows(values, by, seq):
    rows = values.shape[0]
    row = lax.broadcasted_iota(jnp.int32, values.shape, 0)
    if by > 0:
        keep = (row >= by) & ((row < seq) | (row >= seq + by))
        turned = pltpu.roll(values, by, 0)
    else:
        keep = (row < rows + by) & ((row < seq + by) | (row >= seq))
        turned = pltpu.roll(values, rows + by, 0)
    return jnp.where(keep, turned, 0.0)


def conv_backward(
    seq, acc_ref, slope_ref, rows_ref, taps_ref, inner_ref, vals_ref, grads_ref, active=None, kept_ref=None
):
    rows, channels = acc_ref.shape
    lags = taps_ref.shape[0]
    block = 256 if channels % 256 == 0 else LANES
    sums = jnp.zeros((rows, LANES), F32)

    def set_grads(lag, part, value):
        row = slice(lag, lag + 1)
        if kept_ref is not None:
            value = jnp.where(active, value, kept_ref[row, part])
        grads_ref[row, part] = value

    for at in range(0, channels, block):
        part = slice(at, at + block)
        d_pre = acc_ref[:, part] * slope_ref[:, part]
        values = rows_ref[:, part]
        d_vals = taps_ref[0:1, part] * d_pre
        set_grads(0, part, jnp.sum(d_pre * values, axis=0, keepdims=True))
        for lag in range(1, lags):
            ahead = moved_rows(d_pre, -lag, seq)
            d_vals = d_vals + taps_ref[lag : lag + 1, part] * ahead
            set_grads(lag, part, jnp.sum(ahead * values, axis=0, keepdims=True))
        rounded = d_vals.astype(BF16)
        vals_ref[:, part] = rounded
        if inner_ref is None:
            continue
        product = rounded.astype(F32) * inner_ref[:, part]
        for lane in range(0, block, LANES):
            sums = sums + product[:, lane : lane + LANES]
    return jnp.broadcast_to(jnp.sum(sums, axis=1, keepdims=True), (rows, LANES))


def first_kernel(
    seq,
    me_slot,
    sections,
    idx_ref,
    *refs,
):
    sources, refs = refs[:7], refs[7:]
    wo_hbm, wi_hbm, *refs = refs
    vals_ref, grads_ref, sums_ref, inner_ref, slope_ref, rows_ref, *refs = refs
    normed_ref, inv_ref, up_ref, gain_part_ref, *refs = refs
    full_ref, *refs = refs
    flag_refs, refs = refs[:sections], refs[sections:]
    weights, refs = refs[:-11], refs[-11:]
    counts_ref, dy_ref, mask_ref, layer_ref, conv_ref, gain_ref, taps_ref, *refs = refs
    top_ref, scaled_ref, acc_ref, sem = refs
    blocks = len(weights) // 2
    wo_refs, wi_refs = weights[:blocks], weights[blocks:]
    model = gain_ref.shape[1]
    width = up_ref.shape[1]
    lags, channels = taps_ref.shape
    rows = acc_ref.shape[0]
    short = rows - seq

    def columns(i):
        return pl.ds(pl.multiple_of(idx_ref[me_slot + i] * width, width), width)

    held = [counts_ref, mask_ref, dy_ref, layer_ref, conv_ref, gain_ref, taps_ref]
    small = [
        pltpu.make_async_copy(source, ref, sem.at[2 * blocks + i])
        for i, (source, ref) in enumerate(zip(sources, held))
    ]
    out_copies = [
        pltpu.make_async_copy(wo_hbm.at[:, columns(i)], wo_refs[i], sem.at[i])
        for i in range(blocks)
    ]
    in_copies = [
        pltpu.make_async_copy(wi_hbm.at[columns(blocks + i), :], wi_refs[i], sem.at[blocks + i])
        for i in range(blocks)
    ]
    steps = [(outer, i) for i in range(blocks) for outer in (True, False)]
    order = small[:3] + out_copies[:1] + small[3:]
    order += [(out_copies if outer else in_copies)[i] for outer, i in steps[1:]]
    for copy in order:
        copy.start()

    for step, flag_ref in enumerate(flag_refs):
        flag = jnp.where(idx_ref[me_slot + 2 * blocks + step] == 1, 1.0, 0.0)
        flag_ref[...] = jnp.full(flag_ref.shape, flag, F32)
    small[0].wait()
    full = jnp.where(counts_ref[0] == seq, 0, 1)
    full_ref[...] = jnp.full(full_ref.shape, jnp.where(full == 1, 1.0, 0.0), F32)

    def live(ref, part):
        head = ref[full, :, part].astype(F32)
        tail = ref[1 - full, :short, part].astype(F32)
        return jnp.concatenate([head, tail], axis=0)

    def keep_column(batch):
        lane = lax.broadcasted_iota(jnp.int32, (seq, seq), 1)
        row = lax.broadcasted_iota(jnp.int32, (seq, seq), 0)
        mask = jnp.broadcast_to(mask_ref[pl.ds(batch, 1), :], (seq, seq))
        on = (mask == 1) & (lane < counts_ref[batch]) & (lane == row)
        return jnp.sum(jnp.where(on, 1.0, 0.0), axis=1, keepdims=True)

    small[1].wait()
    keep = jnp.concatenate([keep_column(full), keep_column(1 - full)[:short]], axis=0)

    def make_top(i):
        top_ref[i] = (live(dy_ref, columns(i)) * keep).astype(BF16)

    block = 256 if channels % 256 == 0 else LANES
    slope_parts = list(range(0, channels, block))

    def make_slope(at):
        part = slice(at, at + block)
        values = live(conv_ref, part)
        rows_ref[:, part] = values
        pre_act = taps_ref[0:1, part] * values
        for lag in range(1, lags):
            pre_act = pre_act + taps_ref[lag : lag + 1, part] * moved_rows(values, lag, seq)
        gate = 1.0 / (1.0 + jnp.exp(-pre_act))
        slope_ref[:, part] = gate * (1.0 + pre_act * (1.0 - gate))

    def make_scaled(i):
        part = columns(blocks + i)
        scaled_ref[i % 2] = (live(layer_ref, part) * gain_ref[:, part]).astype(BF16)

    small[2].wait()
    make_top(0)
    up_ref[...] = top_ref[0]
    squares = jnp.zeros((rows, LANES), F32)
    for outer, i in steps:
        if outer:
            out_copies[i].wait()
            for at in range(0, channels, block):
                part = slice(at, at + block)
                term = lax.dot_general(
                    top_ref[i], wo_refs[i][part, :], NT, preferred_element_type=F32
                )
                acc_ref[:, part] = term if i == 0 else acc_ref[:, part] + term
            if i == 0:
                for copy in small[3:]:
                    copy.wait()
                make_scaled(0)
            if i + 1 < blocks:
                make_top(i + 1)
            values = live(layer_ref, slice(i * width, (i + 1) * width))
            values = values * values
            for lane in range(0, width, LANES):
                squares = squares + values[:, lane : lane + LANES]
            for at in slope_parts[i::blocks]:
                make_slope(at)
            if i == blocks - 1:
                conv_backward(seq, acc_ref, slope_ref, rows_ref, taps_ref, None, vals_ref, grads_ref)
        else:
            in_copies[i].wait()
            for at in range(0, channels, block):
                part = slice(at, at + block)
                term = lax.dot_general(
                    scaled_ref[i % 2], wi_refs[i][:, part], NN, preferred_element_type=F32
                )
                inner_ref[:, part] = term if i == 0 else inner_ref[:, part] + term
            if i + 1 < blocks:
                make_scaled(i + 1)
    mean = jnp.sum(squares, axis=1, keepdims=True) * (1.0 / model)
    inv = lax.rsqrt(mean + EPSILON)
    inv_ref[...] = jnp.broadcast_to(inv, inv_ref.shape)
    normed_ref[...] = live(layer_ref, columns(0)) * inv
    gain_part_ref[...] = gain_ref[:, columns(0)]
    sums = jnp.zeros((rows, LANES), F32)
    for at in range(0, channels, LANES):
        part = slice(at, at + LANES)
        inner = inner_ref[:, part] * inv
        inner_ref[:, part] = inner
        sums = sums + vals_ref[:, part].astype(F32) * inner
    sums_ref[...] = jnp.broadcast_to(jnp.sum(sums, axis=1, keepdims=True), (rows, LANES))


def act_kernel(seq, count, first, last, *refs):
    pieces, wo_refs, refs = refs[:count], refs[count : 2 * count], refs[2 * count :]
    if not first:
        so_far, refs = refs[0], refs[1:]
    if last:
        slope_ref, rows_ref, taps_ref, inner_ref, kept_ref, working_ref, *refs = refs
        vals_ref, grads_ref, sums_ref, acc_ref = refs
    else:
        (acc_ref,) = refs
    channels = acc_ref.shape[1]
    block = 256 if channels % 256 == 0 else LANES
    for at in range(0, channels, block):
        part = slice(at, at + block)
        total = None if first else so_far[:, part]
        for piece, wo_ref in zip(pieces, wo_refs):
            term = lax.dot_general(piece[...], wo_ref[part, :], NT, preferred_element_type=F32)
            total = term if total is None else total + term
        acc_ref[:, part] = total
    if last:
        active = working_ref[0:1, 0:1] > 0.0
        sums_ref[...] = conv_backward(
            seq, acc_ref, slope_ref, rows_ref, taps_ref, inner_ref, vals_ref, grads_ref, active, kept_ref
        )


def block_product(vals_ref, wi_ref, at, chunk):
    return lax.dot_general(
        vals_ref[...], wi_ref[at : at + chunk, :], NT, preferred_element_type=F32
    )


def split_sums(sums):
    high = sums.astype(BF16)
    low = (sums - high.astype(F32)).astype(BF16)
    lane = lax.broadcasted_iota(jnp.int32, sums.shape, 1)
    return jnp.where(lane < LANES // 2, high.astype(F32), low.astype(F32)).astype(BF16)


def joined_sums(block, width):
    high = block[:, width : width + 1].astype(F32)
    return high + block[:, width + LANES // 2 : width + LANES // 2 + 1].astype(F32)


def other_blocks_kernel(vals_ref, sums_ref, *refs):
    wi_refs, out_ref = refs[:-1], refs[-1]
    width = out_ref.shape[2] - LANES
    chunk = min(512, width)
    for number, wi_ref in enumerate(wi_refs):
        for at in range(0, width, chunk):
            term = block_product(vals_ref, wi_ref, at, chunk)
            out_ref[number, :, at : at + chunk] = term.astype(BF16)
        out_ref[number, :, width:] = split_sums(sums_ref[...])


def own_blocks_kernel(chips, picks, vals_ref, sums_ref, *refs):
    count = len(chips)
    wi_refs, recv_refs, out_refs = refs[:count], refs[count:-count], refs[-count:]
    width = out_refs[0].shape[1] - LANES
    chunk = min(512, width)
    for chip, pick, wi_ref, out_ref in zip(chips, picks, wi_refs, out_refs):
        for at in range(0, width, chunk):
            term = block_product(vals_ref, wi_ref, at, chunk)
            for number, slot in pick:
                part = slice(at, at + chunk)
                recv = recv_refs[number]
                recv = recv[:, part] if slot is None else recv[slot, :, part]
                term = term + recv.astype(F32)
            out_ref[:, at : at + chunk] = term.astype(out_ref.dtype)
        sums = sums_ref[...]
        for number, slot in pick:
            recv = recv_refs[number]
            sums = sums + joined_sums(recv if slot is None else recv.at[slot], width)
        out_ref[:, width:] = split_sums(sums) if chip else sums


def norm_kernel(
    model,
    first,
    last,
    own_ref,
    a_ref,
    b_ref,
    normed_ref,
    inv_ref,
    gain_ref,
    up_ref,
    *refs,
):
    if not first:
        earlier_ref, gains_ref, working_ref, *refs = refs
        active = working_ref[0:1, 0:1] > 0.0
    if last:
        (out_ref,) = refs
    else:
        out_ref, kept_ref, sum_ref = refs
    rows, width = normed_ref.shape
    sums = own_ref[:, width : width + 1]
    for ref in (a_ref, b_ref):
        sums = sums + joined_sums(ref, width)
    mean = sums * (1.0 / model)
    inv = inv_ref[:, 0:1]
    chunk = min(512, width)
    for at in range(0, width, chunk):
        part = slice(at, at + chunk)
        d_norm = own_ref[:, part]
        for ref in (a_ref, b_ref):
            d_norm = d_norm + ref[:, part].astype(F32)
        normed = normed_ref[:, part]
        d_in = inv * (d_norm * gain_ref[:, part] - normed * mean)
        grad = up_ref[:, part].astype(F32) + d_in
        gains = jnp.sum(d_norm * normed, axis=0, keepdims=True)
        kept = grad
        if not first:
            kept = jnp.where(active, grad, earlier_ref[:, part].astype(F32))
            gains = jnp.where(active, gains, gains_ref[:, part])
        if last:
            high = gains.astype(BF16).astype(F32)
            row = lax.broadcasted_iota(jnp.int32, (GAIN_ROWS, chunk), 0)
            both = jnp.where(row == 0, high, jnp.where(row == 1, gains - high, 0.0))
            out_ref[:rows, part] = kept.astype(BF16)
            out_ref[rows:, part] = both.astype(BF16)
        else:
            out_ref[:, part] = grad.astype(BF16)
            kept_ref[:, part] = kept.astype(BF16)
            sum_ref[:, part] = gains


def assemble_kernel(seq, rows, distances, first, full_ref, *refs):
    if not first:
        refs = refs[2:]
    pieces, (out_ref, gain_ref, zero_ref, sem) = refs[:-4], refs[-4:]
    me = lax.axis_index("tensor")
    width = pieces[0].shape[1]
    full = jnp.where(jnp.max(full_ref[...]) > 0.5, 1, 0)
    short = rows - seq
    copies = []
    if first:
        zero_ref[...] = jnp.zeros(zero_ref.shape, BF16)
        copies.append(pltpu.make_async_copy(zero_ref, out_ref.at[1 - full, short:], sem.at[0]))
    for distance, piece in zip(distances, pieces):
        columns = pl.ds(pl.multiple_of((me ^ distance) * width, width), width)
        ends = (
            (piece.at[:seq], out_ref.at[full, :, columns]),
            (piece.at[seq:rows], out_ref.at[1 - full, :short, columns]),
        )
        for source, target in ends:
            copies.append(pltpu.make_async_copy(source, target, sem.at[len(copies)]))
    for copy in copies:
        copy.start()
    for distance, piece in zip(distances, pieces):
        gains = piece[rows:].astype(F32)
        gain_ref[pl.ds(me ^ distance, 1), :] = gains[0:1] + gains[1:2]
    for copy in copies:
        copy.wait()


def local(dy_top, loss_mask, counts, layer_in, conv_in, norm_gain, conv_weight, in_proj, out_proj):
    sections = lax.axis_size("section")
    tensors = lax.axis_size("tensor")
    section = lax.axis_index("section").astype(jnp.int32)
    me = lax.axis_index("tensor").astype(jnp.int32)
    seq, model = dy_top.shape[1:]
    short = seq // 2
    rows = seq + short
    parts = tensors // CHIPS
    width = model // tensors
    w_in, w_out, taps = in_proj[0], out_proj[0], conv_weight[0]
    lags, channels = taps.shape

    me_slot = 0

    blocks = jnp.arange(tensors, dtype=jnp.int32) ^ me
    roles = []
    for role in range(CHIPS):
        for side in range(parts):
            device = me ^ side
            odd = device & 1
            hop = {0: 0, 1: 1 + odd, 2: 2 - odd, 3: 3}[role]
            roles.append(device ^ (hop * parts))
    working = (jnp.arange(sections) == sections - 1 - section).astype(jnp.int32)
    table = jnp.concatenate([blocks, jnp.stack(roles), working])

    def across(x, chip):
        return lax.ppermute(x, "tensor", [(i, i ^ (chip * parts)) for i in range(tensors)])

    def first_hop(x):
        pairs = [(i, i ^ (2 * parts if i % 2 else parts)) for i in range(tensors)]
        return lax.ppermute(x, "tensor", pairs)

    def second_hop(x):
        pairs = [(i, i ^ (parts if i % 2 else 2 * parts)) for i in range(tensors)]
        return lax.ppermute(x, "tensor", pairs)

    def sideways(x, side):
        return lax.ppermute(x, "tensor", [(i, i ^ side) for i in range(tensors)])

    def below(x):
        return lax.ppermute(x, "section", [(i, i - 1) for i in range(1, sections)])

    sides = range(1, parts)
    order = (3, 1, 2)

    def product_cost(count, as_rows=512):
        return dict(
            flops=2 * as_rows * channels * width * count,
            moved=2 * channels * width * count,
        )

    vals_shape = SDS((rows, channels), BF16)
    grads_shape = SDS((lags, channels), F32)
    sums_shape = SDS((rows, LANES), F32)
    channel_shape = SDS((rows, channels), F32)
    block_rows = [(channels, width)] * tensors + [(width, channels)] * tensors
    d_vals, tap_grads, sums, inner, slope, conv_rows, normed, inv, upstream, gain, *rest = kernel_call(
        functools.partial(first_kernel, seq, me_slot, sections),
        (
            vals_shape,
            grads_shape,
            sums_shape,
            channel_shape,
            channel_shape,
            channel_shape,
            SDS((rows, width), F32),
            SDS((rows, LANES), F32),
            SDS((rows, width), BF16),
            SDS((1, width), F32),
        )
        + (SDS((8, LANES), F32),) * (1 + sections)
        + tuple(pltpu.VMEM(shape, BF16) for shape in block_rows),
        [table]
        + [
            pltpu.with_memory_space_constraint(source, pltpu.HBM)
            for source in (
                counts, loss_mask, dy_top, layer_in[0], conv_in[0], norm_gain, taps, w_out, w_in
            )
        ],
        [
            pltpu.SMEM(counts.shape, jnp.int32),
            pltpu.VMEM(dy_top.shape, BF16),
            pltpu.VMEM(loss_mask.shape, jnp.int32),
            pltpu.VMEM(layer_in.shape[1:], BF16),
            pltpu.VMEM(conv_in.shape[1:], BF16),
            pltpu.VMEM(norm_gain.shape, F32),
            pltpu.VMEM(taps.shape, F32),
            pltpu.VMEM((tensors, rows, width), BF16),
            pltpu.VMEM((2, rows, width), BF16),
            pltpu.VMEM((rows, channels), F32),
            pltpu.SemaphoreType.DMA((2 * tensors + 7,)),
        ],
        limit=12,
        flops=4 * rows * channels * model,
        moved=4 * channels * model,
        specs=[SMEM] + [HBM] * 9,
    )
    full, *rest = rest
    flags, weights = rest[:sections], rest[sections:]
    wo, wi = weights[:tensors], weights[tensors:]

    def activation(step, own, taps_kept):
        far = {chip: across(own, chip) for chip in order}
        far[0] = own
        plan = (0,) + order
        total, waiting = None, []
        for number in range(len(plan) + 1):
            first, last = number == 0, number == len(plan)
            group, waiting = waiting, []
            if not last:
                chip = plan[number]
                piece = far[chip]
                if not first:
                    piece, total = lax.optimization_barrier((piece, total))
                group.append((piece, chip, 0))
                waiting = [(sideways(piece, side), chip, side) for side in sides]
            operands = [piece for piece, _, _ in group]
            operands += [resident(wo[chip * parts + side]) for _, chip, side in group]
            operands += [] if first else [total]
            operands += [slope, conv_rows, taps, inner, taps_kept, flags[step]] if last else []
            total = kernel_call(
                functools.partial(act_kernel, seq, len(group), first, last),
                (vals_shape, grads_shape, sums_shape) if last else channel_shape,
                operands,
                [pltpu.VMEM((rows, channels), F32)] if last else [],
                **product_cost(len(group), 512),
            )
        return total

    def summed(vals, row_sums):
        def for_others(chips, after=None):
            return [
                sideways(
                    kernel_call(
                        other_blocks_kernel,
                        SDS((len(chips), rows, width + LANES), BF16),
                        [vals, row_sums] + [resident(wi[chip * parts + side]) for chip in chips],
                        after=after,
                        **product_cost(len(chips), 64),
                    ),
                    side,
                )
                for side in sides
            ]

        def for_own(chips, batches, after=None, arrays=()):
            arrays = list(arrays)
            picks = [[(number, None) for number in range(len(arrays))] for _ in chips]
            for batch_chips, batch in batches:
                for array in batch:
                    for slot, chip in enumerate(batch_chips):
                        if chip in chips:
                            picks[chips.index(chip)].append((len(arrays), slot))
                    arrays.append(array)
            return kernel_call(
                functools.partial(own_blocks_kernel, chips, picks),
                tuple(SDS((rows, width + LANES), BF16 if chip else F32) for chip in chips),
                [vals, row_sums] + [resident(wi[chip * parts]) for chip in chips] + arrays,
                after=after,
                **product_cost(len(chips), 64),
            )

        early, late = (order[0], order[1]), order[2:]
        sent_early = (early, for_others(early))
        sent_late = (late, for_others(late))
        (third,) = for_own(order[:1], [sent_early])
        passing = first_hop(third)
        (first,) = for_own(order[1:2], [sent_early], third)
        (second,) = for_own(order[2:], [sent_late], first, [passing])
        (own,) = for_own((0,), [((0,), for_others((0,), first))], second)
        return own, first_hop(first), second_hop(second)

    taps_kept = tap_grads
    for step in range(sections):
        first, last = step == 0, step == sections - 1
        if not first:
            d_vals, taps_kept, sums = activation(step, upstream, taps_kept)
        terms = summed(d_vals, sums)
        block = SDS((rows, width), BF16)
        results = kernel_call(
            functools.partial(norm_kernel, model, first, last),
            SDS((rows + GAIN_ROWS, width), BF16) if last else (block, block, SDS((1, width), F32)),
            list(terms) + [normed, inv, gain, upstream] + ([] if first else [kept, gains, flags[step]]),
        )
        if last:
            own = results
        else:
            grad, kept, gains = results
            upstream = below(grad)

    far = {chip: across(own, chip) for chip in order}
    far[0] = own
    pieces = {
        (chip, side): sideways(far[chip], side) if side else far[chip]
        for chip in (0,) + order
        for side in range(parts)
    }
    early = [(0, side) for side in range(parts)] + [(order[0], 0)]
    late = [key for key in pieces if key not in early]
    results = []
    for keys in (early, late):
        results = kernel_call(
            functools.partial(
                assemble_kernel, seq, rows, [c * parts + side for c, side in keys], not results
            ),
            (SDS((2, seq, model), BF16), SDS((tensors, width), F32)),
            [full] + list(results) + [pieces[key] for key in keys],
            [
                pltpu.VMEM((seq - short, model), BF16),
                pltpu.SemaphoreType.DMA((2 * len(keys) + 1,)),
            ],
            specs=[VMEM] + ([HBM, VMEM] if results else []) + [VMEM] * len(keys),
            out_specs=(HBM, VMEM),
            aliases={1: 0, 2: 1} if results else {},
        )
    result, gain_grads = results[0], results[1].reshape(1, model)
    return (result[None], gain_grads, taps_kept[None])


def solution(mesh):
    placed = (
        P(),
        P(),
        P(),
        P("section", None, None, None),
        P("section", None, None, "tensor"),
        P("section", None),
        P("section", None, "tensor"),
        P("section", None, "tensor"),
        P("section", "tensor", None),
    )
    return jax.shard_map(
        local,
        mesh=mesh,
        in_specs=placed,
        out_specs=(
            P("section", None, None, None),
            P("section", None),
            P("section", None, "tensor"),
        ),
        check_vma=False,
    )
```
